128 devices in a mesh: ctx: 64 (over y, x, z), tp: 2 (over core).
Axes of the slice: x: 4, y: 4, z: 4, core: 2. Of those that a mesh axis runs over, the one named last changes fastest.
Arguments:
- tokens: bfloat16 [64, 2, 80, 896], P('ctx', None, 'tp'), may hold values from -16 to 16
- gain_attn: float32 [896], replicated, may hold values from 0.5 to 1.5
- query_projection_weight: bfloat16 [896, 896], P(None, 'tp'), may hold values from -0.1875 to 0.1875
- query_bias_vector: float32 [896], P('tp'), may hold values from -3 to 3
- key_projection_weight: bfloat16 [896, 128], P(None, 'tp'), may hold values from -0.1875 to 0.1875
- key_bias_vector: float32 [128], P('tp'), may hold values from -4 to 4
- value_projection_weight: bfloat16 [896, 128], P(None, 'tp'), may hold values from -0.1875 to 0.1875
- value_bias_vector: float32 [128], P('tp'), may hold values from -3 to 3
- w_output: bfloat16 [896, 896], P('tp'), may hold values from -0.75 to 0.75
- gain_mlp: float32 [896], replicated, may hold values from 0.5 to 1.5
- w_gate: bfloat16 [896, 4864], P(None, 'tp'), may hold values from -0.1875 to 0.1875
- w_up: bfloat16 [896, 4864], P(None, 'tp'), may hold values from -0.1875 to 0.1875
- w_down: bfloat16 [4864, 896], P('tp'), may hold values from -0.078125 to 0.078125
- cotangent: bfloat16 [64, 2, 80, 896], P('ctx', None, 'tp'), may hold values from -16 to 16
Outputs:
- mixed: bfloat16 [64, 2, 80, 896], P('ctx', None, 'tp')
- grad_tokens: bfloat16 [64, 2, 80, 896], P('ctx', None, 'tp')
- grad_gain_attn: float32 [896], replicated
- grad_w_query: float32 [896, 896], P('ctx', 'tp')
- grad_b_query: float32 [896], replicated
- grad_w_key: float32 [896, 128], P('ctx', 'tp')
- grad_b_key: float32 [128], replicated
- grad_w_value: float32 [896, 128], P('ctx', 'tp')
- grad_b_value: float32 [128], replicated
- grad_w_output: float32 [896, 896], P('tp', 'ctx')
- grad_gain_mlp: float32 [896], replicated
- grad_w_gate: float32 [896, 4864], P('ctx', 'tp')
- grad_w_up: float32 [896, 4864], P('ctx', 'tp')
- grad_w_down: float32 [4864, 896], P('tp', 'ctx')
The draws below stay inside these ranges and needn't reach their ends.
All inputs are finite; a program needn't handle non-finite values.
Results may differ from the reference program's by a relative error of at most 0.025.
Values may be sent and summed in bfloat16 or wider, within the bound.
No kernel may reach another device: no remote copies, remote signals or barrier semaphores. Data moves between devices by JAX's collectives and lax.ppermute only.
A program may use at most 192 MiB of HBM per device.

```python
import math
import jax
import jax.numpy as jnp
from jax import lax

MODEL_DIM = 896
QUERY_HEADS = 14
KEY_VALUE_HEADS = 2
HEAD_DIM = 64
FF = 4864
BLK = 80
N_CTX = 64


def with_spikes(values, key, source, target, parts, factor):
    owner, partner = [(jnp.arange(values.shape[dim]) // (values.shape[dim] // parts)).reshape([-1 if axis == dim else 1 for axis in range(values.ndim)]) for dim in (source, target)]
    chosen = jax.random.permutation(key, parts)[partner]
    strong = (owner == chosen) | (owner == (partner + parts // 2) % parts)
    return jnp.where(strong, factor * values, values)


def block_scale(stream_key, dims, shards, least, high):
    level = 1.0
    for dim, blocks in shards:
        heights = jax.random.uniform(jax.random.fold_in(jax.random.fold_in(stream_key, 6), dim), (blocks,), jnp.float32, least / len(shards), high / len(shards))
        level = level * jnp.repeat(jnp.exp(heights), dims[dim] // blocks).reshape((-1,) + (1,) * (len(dims) - 1 - dim))
    return level


def scatter_about(own_key, shape, scale, bound, cuts=(), kind=jnp.bfloat16):
    level = block_scale(own_key, shape, cuts, -0.22, 0.18) if cuts else 1.0
    array = jax.random.normal(own_key, shape, jnp.float32) * scale * level
    return jnp.minimum(jnp.maximum(array, -bound), bound).astype(kind)


def bell_draw_with(own_key, dims, scale, limit, cuts, heavy, dtype=jnp.bfloat16):
    values = scale * jax.random.normal(own_key, dims, jnp.float32)
    if cuts:
        values = values * block_scale(own_key, dims, cuts, -0.22, 0.18)
    return jnp.clip(with_spikes(values, jax.random.fold_in(own_key, 3), *heavy), -limit, limit).astype(dtype)


def setup_inputs(seed: int = 0) -> dict:
    arg_keys = jax.random.split(jax.random.key(seed), 15)
    tokens = bell_draw_with(arg_keys[0], (N_CTX, 2, BLK, MODEL_DIM), 1.0, 16.0, ((0, 64), (2, 2)), (0, 3, 64, 4.0))
    gain_attn = jnp.clip(1.0 + 0.1 * jax.random.normal(arg_keys[1], (MODEL_DIM,), jnp.float32), 0.5, 1.5)
    query_projection_weight = scatter_about(arg_keys[2], (MODEL_DIM, QUERY_HEADS * HEAD_DIM), MODEL_DIM ** -0.5, 0.1875, ((1, 2),))
    query_bias_vector = scatter_about(arg_keys[3], (QUERY_HEADS * HEAD_DIM,), 0.5, 3.0, ((0, 2),), jnp.float32)
    key_projection_weight = scatter_about(arg_keys[4], (MODEL_DIM, KEY_VALUE_HEADS * HEAD_DIM), MODEL_DIM ** -0.5, 0.1875, ((1, 2),))
    key_bias_vector = scatter_about(arg_keys[5], (KEY_VALUE_HEADS * HEAD_DIM,), 1.0, 4.0, ((0, 2),), jnp.float32)
    value_projection_weight = scatter_about(arg_keys[6], (MODEL_DIM, KEY_VALUE_HEADS * HEAD_DIM), MODEL_DIM ** -0.5, 0.1875, ((1, 2),))
    value_bias_vector = scatter_about(arg_keys[7], (KEY_VALUE_HEADS * HEAD_DIM,), 0.5, 3.0, ((0, 2),), jnp.float32)
    w_output = scatter_about(arg_keys[8], (QUERY_HEADS * HEAD_DIM, MODEL_DIM), (QUERY_HEADS * HEAD_DIM // 16) ** -0.5, 0.75, ((0, 2),))
    gain_mlp = jnp.clip(1.0 + 0.1 * jax.random.normal(arg_keys[9], (MODEL_DIM,), jnp.float32), 0.5, 1.5)
    w_gate = scatter_about(arg_keys[10], (MODEL_DIM, FF), MODEL_DIM ** -0.5, 0.1875, ((1, 2),))
    w_up = scatter_about(arg_keys[11], (MODEL_DIM, FF), MODEL_DIM ** -0.5, 0.1875, ((1, 2),))
    w_down = scatter_about(arg_keys[12], (FF, MODEL_DIM), FF ** -0.5, 0.078125, ((0, 2),))
    cotangent = bell_draw_with(arg_keys[13], (N_CTX, 2, BLK, MODEL_DIM), 1.0, 16.0, ((0, 64), (2, 2)), (0, 3, 64, 4.0))
    return {"tokens": tokens, "gain_attn": gain_attn, "query_projection_weight": query_projection_weight, "query_bias_vector": query_bias_vector, "key_projection_weight": key_projection_weight, "key_bias_vector": key_bias_vector, "value_projection_weight": value_projection_weight, "value_bias_vector": value_bias_vector, "w_output": w_output, "gain_mlp": gain_mlp, "w_gate": w_gate, "w_up": w_up, "w_down": w_down, "cotangent": cotangent}


EPS = 1e-06
THETA = 1000000.0
HIGH = lax.Precision.HIGHEST

@jax.custom_vjp
def reduced_precision(v):
    return lax.optimization_barrier(v.astype(jnp.bfloat16)).astype(jnp.float32)

@jax.custom_vjp
def reduced_precision_backward(v):
    return v

def low_keep(v):
    return (reduced_precision(v), None)

def low_pass(kept, grad):
    return (grad,)

def back_keep(v):
    return (v, None)

def back_low(kept, grad):
    return (reduced_precision(grad),)
reduced_precision.defvjp(low_keep, low_pass)
reduced_precision_backward.defvjp(back_keep, back_low)

def precise_product(left, right):
    return jnp.dot(left, right, precision=HIGH, preferred_element_type=jnp.float32)

def rms_norm(rows, gain):
    return rows * lax.rsqrt(lax.optimization_barrier(jnp.mean(rows * rows, axis=-1, keepdims=True)) + EPS) * gain

def to_sequence(blocks):
    model_width = blocks.shape[-1]
    early_rows = blocks[:, 0].reshape(-1, model_width)
    late_rows = blocks[::-1, 1].reshape(-1, model_width)
    return jnp.concatenate([early_rows, late_rows], axis=0)

def from_sequence(rows, ctx_count, block_size):
    model_width = rows.shape[-1]
    middle = ctx_count * block_size
    early_rows = rows[:middle].reshape(ctx_count, block_size, model_width)
    late_rows = rows[middle:].reshape(ctx_count, block_size, model_width)[::-1]
    return jnp.stack([early_rows, late_rows], axis=1)

def rope_tables(token_positions, head_size):
    freqs = 1.0 / THETA ** (jnp.arange(0, head_size, 2).astype(jnp.float32) / head_size)
    angles = token_positions.astype(jnp.float32)[:, None] * freqs[None, :]
    return (jnp.cos(angles), jnp.sin(angles))

def rotate(vectors, cosine, sine):
    shape_parts = (vectors.shape[0],) + (1,) * (vectors.ndim - 2) + (vectors.shape[-1] // 2,)
    cosine_part = cosine.reshape(shape_parts)
    sine_part = sine.reshape(shape_parts)
    leading, trailing = jnp.split(vectors, 2, axis=-1)
    return jnp.concatenate([leading * cosine_part - trailing * sine_part, trailing * cosine_part + leading * sine_part], axis=-1)

def forward(x_rows, gain_attn, query_projection_weight, query_bias_vector, key_projection_weight, key_bias_vector, value_projection_weight, value_bias_vector, w_output, gain_mlp, w_gate, w_up, w_down):
    sequence_length = x_rows.shape[0]
    query_group_width = QUERY_HEADS // KEY_VALUE_HEADS
    token_positions = jnp.arange(sequence_length)
    cosine, sine = rope_tables(token_positions, HEAD_DIM)
    normalized_rows = reduced_precision(rms_norm(x_rows, gain_attn))
    projected_queries = reduced_precision_backward(precise_product(normalized_rows, query_projection_weight) + query_bias_vector).reshape(sequence_length, KEY_VALUE_HEADS, query_group_width, HEAD_DIM)
    projected_keys = reduced_precision_backward(precise_product(normalized_rows, key_projection_weight) + key_bias_vector).reshape(sequence_length, KEY_VALUE_HEADS, HEAD_DIM)
    projected_values = reduced_precision(reduced_precision_backward(precise_product(normalized_rows, value_projection_weight) + value_bias_vector)).reshape(sequence_length, KEY_VALUE_HEADS, HEAD_DIM)
    projected_queries = reduced_precision(rotate(projected_queries, cosine, sine))
    projected_keys = reduced_precision(rotate(projected_keys, cosine, sine))
    scale_factor = 1.0 / math.sqrt(HEAD_DIM)
    rows_per_block = math.gcd(sequence_length, 512)
    block_count = sequence_length // rows_per_block

    def attention_forward(pieces):
        query_block, query_places = pieces
        scores = jnp.einsum('qkgd,skd->kgqs', query_block, projected_keys, precision=HIGH, preferred_element_type=jnp.float32) * scale_factor
        allowed = query_places[:, None] >= token_positions[None, :]
        scores = reduced_precision_backward(jnp.where(allowed, scores, -1e+30))
        row_max = lax.optimization_barrier(jnp.max(scores, axis=-1, keepdims=True))
        exponent = jnp.exp(scores - row_max)
        attn_probs = reduced_precision(exponent / lax.optimization_barrier(jnp.sum(exponent, axis=-1, keepdims=True)))
        return jnp.einsum('kgqs,skd->qkgd', attn_probs, projected_values, precision=HIGH, preferred_element_type=jnp.float32)
    output_blocks = lax.map(jax.checkpoint(attention_forward), (projected_queries.reshape(block_count, rows_per_block, KEY_VALUE_HEADS, query_group_width, HEAD_DIM), token_positions.reshape(block_count, rows_per_block)))
    attended = reduced_precision(reduced_precision_backward(output_blocks.reshape(sequence_length, QUERY_HEADS * HEAD_DIM)))
    attn_out = reduced_precision_backward(precise_product(attended, w_output))
    hidden_rows = x_rows + attn_out
    normed_mlp = reduced_precision(rms_norm(hidden_rows, gain_mlp))
    gate_rows = reduced_precision_backward(precise_product(normed_mlp, w_gate))
    up_rows = reduced_precision_backward(precise_product(normed_mlp, w_up))
    activation = reduced_precision(jax.nn.silu(gate_rows) * up_rows)
    mlp_out = reduced_precision_backward(precise_product(activation, w_down))
    return hidden_rows + mlp_out

def reference(tokens, gain_attn, query_projection_weight, query_bias_vector, key_projection_weight, key_bias_vector, value_projection_weight, value_bias_vector, w_output, gain_mlp, w_gate, w_up, w_down, cotangent):
    ctx_count = tokens.shape[0]
    block_size = tokens.shape[2]
    result, pullback = jax.vjp(forward, to_sequence(tokens.astype(jnp.float32)), gain_attn, query_projection_weight.astype(jnp.float32), query_bias_vector, key_projection_weight.astype(jnp.float32), key_bias_vector, value_projection_weight.astype(jnp.float32), value_bias_vector, w_output.astype(jnp.float32), gain_mlp, w_gate.astype(jnp.float32), w_up.astype(jnp.float32), w_down.astype(jnp.float32))
    grads = pullback(to_sequence(cotangent.astype(jnp.float32)))
    mixed = from_sequence(result, ctx_count, block_size).astype(jnp.bfloat16)
    grad_tokens = from_sequence(grads[0], ctx_count, block_size).astype(jnp.bfloat16)
    return (mixed, grad_tokens, grads[1], grads[2], grads[3], grads[4], grads[5], grads[6], grads[7], grads[8], grads[9], grads[10], grads[11], grads[12])
```

```python
import functools

import jax
import jax.numpy as jnp
from jax import lax
from jax.experimental import pallas as pl
from jax.experimental.pallas import tpu as pltpu
from jax.sharding import Mesh
from jax.sharding import PartitionSpec as P

HEAD_DIM = 64
HEADS = 7
HALF = HEAD_DIM // 2
WIDE = 2 * HEAD_DIM
LANES = 640
CHUNK = 4
CTX = ("ctx_0", "ctx_1", "ctx_2")
ORDERS = (
    ("ctx_0", "ctx_1", "ctx_2"),
    ("ctx_1", "ctx_2", "ctx_0"),
    ("ctx_2", "ctx_0", "ctx_1"),
)
SIDE = 4
EPS = 1e-06
THETA = 1000000.0
NEG_FILL = -1e30
BF = jnp.bfloat16
F32 = jnp.float32


def columns_of(rows, group, block):
    parts = [
        rows[group * block : (group + 1) * block, h * HEAD_DIM : (h + 1) * HEAD_DIM]
        for h in range(HEADS)
    ]
    parts.append(jnp.zeros((LANES - HEADS * block, HEAD_DIM), rows.dtype))
    return jnp.concatenate(parts, axis=0)


def rows_of(columns, block):
    return jnp.concatenate(
        [columns[h * block : (h + 1) * block] for h in range(HEADS)], axis=1
    )


def slot_of(j, me_ref):
    return ((j // SIDE - me_ref[0]) & (SIDE - 1)) * SIDE + ((j % SIDE - me_ref[1]) & (SIDE - 1))


def causal(me2, late, block, query_row):
    shape = (CHUNK, block, LANES)
    b = lax.broadcasted_iota(jnp.int32, shape, 0).reshape(CHUNK * block, LANES)
    r = lax.broadcasted_iota(jnp.int32, shape, 1).reshape(CHUNK * block, LANES)
    ahead = (((b + me2) & (CHUNK - 1)) - me2) * block
    ahead = -ahead if late else ahead
    return ahead + r <= query_row


def forward_kernel(
    me_ref, q_ref, early_ref, late_ref, cos_ref, sin_ref, row_ref, qt_ref, ot_ref, lse_ref, att_ref
):
    block = q_ref.shape[0] // 2
    keys = CHUNK * block
    chunks = early_ref.shape[0]
    mine = me_ref[0] * SIDE + me_ref[1]
    lane = lax.broadcasted_iota(jnp.int32, (keys, WIDE), 1)
    for g in (0, 1):
        qt = columns_of(q_ref[...], g, block).T
        u, w = qt[:HALF], qt[HALF:]
        cos, sin = cos_ref[g], sin_ref[g]
        turned = jnp.concatenate([u * cos - w * sin, w * cos + u * sin], axis=0)
        qt_ref[g, :HEAD_DIM] = turned.astype(BF) * BF(0.125)
        qt_ref[g, HEAD_DIM:] = jnp.zeros((HEAD_DIM, LANES), BF)

    def step(g, ref, masked, j, carry):
        top, acc = carry
        kv = ref[slot_of(j, me_ref)].reshape(keys, WIDE)
        s = jnp.dot(kv, qt_ref[g], preferred_element_type=F32)
        if masked:
            s = jnp.where(causal(me_ref[2], g == 1, block, row_ref[...]), s, NEG_FILL)
        new = jnp.maximum(top, jnp.max(s, axis=0, keepdims=True))
        p = jnp.exp(s - new).astype(BF)
        shrink = jnp.exp(top - new)
        ones_v = jnp.where(lane < HEAD_DIM, BF(1), kv)
        more = lax.dot_general(ones_v, p, (((0,), (0,)), ((), ())), preferred_element_type=F32)
        return new, acc * shrink + more

    for g in (0, 1):
        carry = (jnp.full((1, LANES), NEG_FILL, F32), jnp.zeros((WIDE, LANES), F32))
        if g == 0:
            carry = lax.fori_loop(
                0, mine, functools.partial(step, 0, early_ref, False), carry
            )
            carry = step(0, early_ref, True, mine, carry)
        else:
            carry = lax.fori_loop(
                0, chunks, functools.partial(step, 1, early_ref, False), carry
            )
            carry = step(1, late_ref, True, mine, carry)
            carry = lax.fori_loop(
                mine + 1, chunks, functools.partial(step, 1, late_ref, False), carry
            )
        top, acc = carry
        total = acc[0:1]
        out = acc[HEAD_DIM:] / total
        ot_ref[g] = out
        lse_ref[g] = top + jnp.log(total)
        att_ref[g * block : (g + 1) * block] = rows_of(out.T, block).astype(BF)


def backward_kernel(
    me_ref,
    qt_ref,
    ot_ref,
    lse_ref,
    grad_ref,
    early_ref,
    late_ref,
    cos_ref,
    sin_ref,
    row_ref,
    dq_ref,
    de_ref,
    dl_ref,
    sum_ref,
):
    block = grad_ref.shape[0] // 2
    keys = CHUNK * block
    chunks = early_ref.shape[0]
    mine = me_ref[0] * SIDE + me_ref[1]

    def clear(j, unused):
        dl_ref[slot_of(j, me_ref)] = jnp.zeros((CHUNK, block, WIDE), dl_ref.dtype)
        return unused

    lax.fori_loop(0, mine, clear, 0)

    for g in (1, 0):
        qt = qt_ref[g]
        grad = columns_of(grad_ref[...].astype(F32), g, block)
        none = jnp.zeros((LANES, HEAD_DIM), F32)
        grad_rows = jnp.concatenate([none, grad], axis=1)
        grad_t = grad_rows.T
        delta = jnp.sum(grad_t[HEAD_DIM:] * ot_ref[g], axis=0, keepdims=True)
        grad_rows = grad_rows.astype(BF)
        grad_t = grad_t.astype(BF)
        q_rows = qt.astype(F32).T.astype(BF)
        lse = lse_ref[g]

        def step(
            early, masked, j, dqt, g=g, qt=qt, rows=grad_rows, cols=grad_t, q=q_rows, lse=lse, d=delta
        ):
            slot = slot_of(j, me_ref)
            kv = (early_ref if early else late_ref)[slot].reshape(keys, WIDE)
            s = jnp.dot(kv, qt, preferred_element_type=F32)
            p = jnp.exp(s - lse)
            if masked:
                p = jnp.where(causal(me_ref[2], g == 1, block, row_ref[...]), p, 0.0)
            dp = jnp.dot(kv, cols, preferred_element_type=F32)
            ds = (p * (dp - d)).astype(BF)
            dkv = jnp.dot(ds, q, preferred_element_type=F32) + jnp.dot(
                p.astype(BF), rows, preferred_element_type=F32
            )
            dqt = dqt + lax.dot_general(
                kv, ds, (((0,), (0,)), ((), ())), preferred_element_type=F32
            )
            if g == 0:
                dkv = dkv + sum_ref[slot].reshape(keys, WIDE)
            dkv = dkv.reshape(CHUNK, block, WIDE)
            if not early:
                dl_ref[slot] = dkv.astype(dl_ref.dtype)
            elif g == 0:
                de_ref[slot] = dkv.astype(de_ref.dtype)
            else:
                sum_ref[slot] = dkv
            return dqt

        dqt = jnp.zeros((WIDE, LANES), F32)
        if g == 1:
            dqt = lax.fori_loop(0, chunks, functools.partial(step, True, False), dqt)
            dqt = step(False, True, mine, dqt)
            dqt = lax.fori_loop(mine + 1, chunks, functools.partial(step, False, False), dqt)
        else:
            dqt = lax.fori_loop(0, mine, functools.partial(step, True, False), dqt)
            dqt = step(True, True, mine, dqt)
        u, w = dqt[:HALF] * 0.125, dqt[HALF:HEAD_DIM] * 0.125
        cos, sin = cos_ref[g], sin_ref[g]
        dq = jnp.concatenate([u * cos + w * sin, w * cos - u * sin], axis=0).T
        dq_ref[g * block : (g + 1) * block] = rows_of(dq, block).astype(dq_ref.dtype)

    def finish(j, unused):
        slot = slot_of(j, me_ref)
        de_ref[slot] = sum_ref[slot].astype(de_ref.dtype)
        return unused

    lax.fori_loop(mine + 1, chunks, finish, 0)


VMEM = pl.BlockSpec(memory_space=pltpu.VMEM)
SMEM = pl.BlockSpec(memory_space=pltpu.SMEM)
PARAMS = pltpu.CompilerParams(vmem_limit_bytes=40 * 1024 * 1024)


def attend(me, q, early, late, cos, sin, rows):
    own = q.shape[0]
    return pl.pallas_call(
        forward_kernel,
        out_shape=(
            jax.ShapeDtypeStruct((2, WIDE, LANES), BF),
            jax.ShapeDtypeStruct((2, HEAD_DIM, LANES), F32),
            jax.ShapeDtypeStruct((2, 1, LANES), F32),
            jax.ShapeDtypeStruct((own, HEADS * HEAD_DIM), BF),
        ),
        in_specs=[SMEM] + [VMEM] * 6,
        out_specs=(VMEM,) * 4,
        compiler_params=PARAMS,
        cost_estimate=pl.CostEstimate(
            flops=22_000_000_000, bytes_accessed=4_000_000, transcendentals=0
        ),
        name="attend",
    )(me, q, early, late, cos, sin, rows)


def attend_back(me, qt, ot, lse, grad, early, late, cos, sin, rows):
    own = grad.shape[0]
    return pl.pallas_call(
        backward_kernel,
        out_shape=(
            jax.ShapeDtypeStruct((own, HEADS * HEAD_DIM), BF),
            jax.ShapeDtypeStruct(early.shape, BF),
            jax.ShapeDtypeStruct(late.shape, BF),
        ),
        in_specs=[SMEM] + [VMEM] * 9,
        out_specs=(VMEM,) * 3,
        scratch_shapes=[pltpu.VMEM(early.shape, F32)],
        compiler_params=PARAMS,
        cost_estimate=pl.CostEstimate(
            flops=28_000_000_000, bytes_accessed=8_000_000, transcendentals=0
        ),
        name="attend_back",
    )(me, qt, ot, lse, grad, early, late, cos, sin, rows)


def send(array, axis, s):
    return lax.ppermute(array, axis, [(i, (i + s) % SIDE) for i in range(SIDE)])


def fetch(array, axis, s):
    return lax.ppermute(array, axis, [(i, (i - s) % SIDE) for i in range(SIDE)])


def other_core(array):
    return lax.ppermute(array, "tp", [(0, 1), (1, 0)])


def gather(array, axis, dim):
    return jnp.stack([array] + [fetch(array, axis, s) for s in range(1, SIDE)], axis=dim)


def total_of(arrays):
    total = arrays[0].astype(F32)
    for a in arrays[1:]:
        total = total + a.astype(F32)
    return total


def sum_at_owner(pieces, axes):
    for axis in axes[:-1]:
        arrays = [pieces[0]] + [send(pieces[s], axis, s) for s in range(1, SIDE)]
        rows = arrays[0].shape[0] // SIDE
        pieces = [
            total_of([a[s * rows : (s + 1) * rows] for a in arrays]).astype(BF)
            for s in range(SIDE)
        ]
    return total_of([pieces[0]] + [send(pieces[s], axes[-1], s) for s in range(1, SIDE)])


def sum_everywhere(vector):
    for axis in CTX:
        vector = total_of([vector] + [fetch(vector, axis, s) for s in range(1, SIDE)])
    return vector + other_core(vector)


def by_distance(me, order, width):
    each = width // SIDE**3
    place = jnp.arange(width)
    part, within = place // each, place % each
    apart = dict(zip(order, (part // SIDE**2, part // SIDE % SIDE, part % SIDE)))
    d0, d1, d2 = [(me[k] + apart[a]) % SIDE for k, a in enumerate(CTX)]
    feature = ((d0 * SIDE + d1) * SIDE + d2) * each + within
    return (jnp.arange(width)[:, None] == feature[None, :]).astype(BF)


def rearranged(rows, table):
    return jnp.dot(rows, table, preferred_element_type=F32).astype(BF)


def weight_pieces(rows, grads):
    size = rows.shape[1] // SIDE
    return [
        lax.dot_general(
            rows[:, s * size : (s + 1) * size],
            grads,
            (((0,), (0,)), ((), ())),
            preferred_element_type=F32,
        ).astype(BF)
        for s in range(SIDE)
    ]


def rms_forward(rows, gain):
    inverse = lax.rsqrt(jnp.mean(rows * rows, axis=-1, keepdims=True) + EPS)
    return (rows * inverse * gain, inverse)


def rms_backward(rows, inverse, gain, grad_out):
    weighted = grad_out * gain
    inner = jnp.mean(rows * weighted, axis=-1, keepdims=True)
    return inverse * weighted - rows * (inverse * inverse * inverse) * inner


def angles(positions):
    freqs = 1.0 / THETA ** (jnp.arange(0, HEAD_DIM, 2).astype(F32) / HEAD_DIM)
    return positions.astype(F32), freqs


def local(
    tokens,
    gain_attn,
    query_projection_weight,
    query_bias_vector,
    key_projection_weight,
    key_bias_vector,
    value_projection_weight,
    value_bias_vector,
    w_output,
    gain_mlp,
    w_gate,
    w_up,
    w_down,
    cotangent,
):
    me = [lax.axis_index(a) for a in CTX]
    tp = lax.axis_index("tp")
    ctx_count = SIDE**3
    ctx = (me[0] * SIDE + me[1]) * SIDE + me[2]
    half = tokens.shape[2]
    block = 2 * half
    width = tokens.shape[3]
    own = 2 * block
    places = jnp.stack([me[0], me[1], me[2], tp]).astype(jnp.int32)

    def both_halves(array):
        parts = lax.all_gather(array.reshape(2, half, width), "tp", axis=0)
        return jnp.moveaxis(parts, 0, 1).reshape(own, width)

    def own_half(array):
        return lax.dynamic_index_in_dim(
            array.reshape(2, 2, half, width), tp, 1, keepdims=False
        ).reshape(block, width)

    def other_half(array):
        return lax.dynamic_index_in_dim(
            array.reshape(2, 2, half, width), 1 - tp, 1, keepdims=False
        ).reshape(block, width)

    firsts = jnp.stack([ctx * block, (2 * ctx_count - 1 - ctx) * block])
    row = jnp.arange(LANES) % block
    row = jnp.where(jnp.arange(LANES) < HEADS * block, row, 0)
    lane_places, freqs = angles(firsts[:, None] + row[None, :])
    lane_angles = lane_places[:, None, :] * freqs[None, :, None]
    lane_cos, lane_sin = jnp.cos(lane_angles), jnp.sin(lane_angles)
    own_places, freqs = angles((firsts[:, None] + jnp.arange(block)[None, :]).reshape(-1))
    own_angles = own_places[:, None] * freqs[None, :]
    cos, sin = jnp.cos(own_angles), jnp.sin(own_angles)
    query_row = row.astype(jnp.int32)[None, :]

    x_all = both_halves(tokens).astype(F32)
    n1, inverse_attn = rms_forward(x_all, gain_attn)
    n1 = n1.astype(BF)
    key_pre = jnp.dot(n1, key_projection_weight, preferred_element_type=F32) + key_bias_vector
    value_pre = jnp.dot(n1, value_projection_weight, preferred_element_type=F32) + value_bias_vector
    u, w = key_pre[:, :HALF], key_pre[:, HALF:]
    kv_own = jnp.concatenate([u * cos - w * sin, w * cos + u * sin, value_pre], axis=1)
    kv_own = kv_own.astype(BF).reshape(2, block, WIDE)
    kv_row = gather(kv_own, "ctx_2", 1)
    early = gather(gather(kv_row[0], "ctx_1", 0), "ctx_0", 0)
    late = gather(gather(kv_row[1], "ctx_0", 0), "ctx_1", 1)
    shape = (SIDE * SIDE, CHUNK, block, WIDE)
    early, late = early.reshape(shape), late.reshape(shape)

    query_pre = (
        jnp.dot(n1, query_projection_weight, preferred_element_type=F32) + query_bias_vector
    )
    dy_all = both_halves(cotangent)
    tables = [by_distance(me, order, width) for order in ORDERS]
    grad_act = jnp.einsum("rd,fd->rf", dy_all, w_down, preferred_element_type=F32)
    dy_2 = rearranged(dy_all, tables[2])
    n1_1 = rearranged(n1, tables[1])
    n1_0 = rearranged(n1, tables[0])

    qt, ot, lse, attended = attend(places, query_pre, early, late, lane_cos, lane_sin, query_row)
    attn_term = jnp.dot(attended, w_output, preferred_element_type=F32).astype(BF)
    attn_rows = attn_term.astype(F32) + other_core(attn_term).astype(F32)
    hidden = x_all + attn_rows

    n2, inverse_mlp = rms_forward(hidden, gain_mlp)
    n2 = n2.astype(BF)
    gate_rows = jnp.dot(n2, w_gate, preferred_element_type=F32)
    up_rows = jnp.dot(n2, w_up, preferred_element_type=F32)
    sigmoid_gate = jax.nn.sigmoid(gate_rows)
    silu_gate = gate_rows * sigmoid_gate
    activation = (silu_gate * up_rows).astype(BF)
    grad_gate = (
        grad_act * up_rows * sigmoid_gate * (1.0 + gate_rows * (1.0 - sigmoid_gate))
    ).astype(BF)
    grad_up = (grad_act * silu_gate).astype(BF)
    down_pieces = weight_pieces(dy_2, activation)
    gate_pieces = weight_pieces(rearranged(n2, tables[0]), grad_gate)
    up_pieces = weight_pieces(rearranged(n2, tables[1]), grad_up)
    dn2_term = (
        jnp.einsum("rf,df->rd", grad_gate, w_gate, preferred_element_type=F32)
        + jnp.einsum("rf,df->rd", grad_up, w_up, preferred_element_type=F32)
    ).astype(BF)
    dn2 = dn2_term.astype(F32) + other_core(dn2_term).astype(F32)
    mlp_term = jnp.dot(activation, w_down, preferred_element_type=F32).astype(BF)
    mlp_rows = own_half(mlp_term).astype(F32) + other_core(other_half(mlp_term)).astype(F32)
    mixed = (own_half(hidden) + mlp_rows).astype(BF).reshape(tokens.shape)

    grad_hidden = dy_all.astype(F32) + rms_backward(hidden, inverse_mlp, gain_mlp, dn2)
    grad_gain_mlp = jnp.sum(dn2 * hidden * inverse_mlp, axis=0)
    grad_attn = grad_hidden.astype(BF)
    grad_attended = jnp.einsum(
        "rd,qd->rq", grad_attn, w_output, preferred_element_type=F32
    ).astype(BF)
    output_pieces = weight_pieces(rearranged(grad_attn, tables[2]), attended)
    gate_shard = sum_at_owner(gate_pieces, ORDERS[0])
    up_shard = sum_at_owner(up_pieces, ORDERS[1])
    down_shard = sum_at_owner(down_pieces, ORDERS[2]).T
    output_shard = sum_at_owner(output_pieces, ORDERS[2]).T

    grad_query, grad_early, grad_late = attend_back(
        places, qt, ot, lse, grad_attended, early, late, lane_cos, lane_sin, query_row
    )
    cube = (SIDE, SIDE, CHUNK, block, WIDE)
    flat = (SIDE * CHUNK, block, WIDE)
    grad_early, grad_late = grad_early.reshape(cube), grad_late.reshape(cube)
    own_early = sum_at_owner([grad_early[s].reshape(flat) for s in range(SIDE)], CTX)
    own_late = sum_at_owner(
        [grad_late[:, s].reshape(flat) for s in range(SIDE)], ("ctx_1", "ctx_0", "ctx_2")
    )
    grad_kv = jnp.concatenate([own_early, own_late], axis=0).reshape(own, WIDE)
    u, w = grad_kv[:, :HALF], grad_kv[:, HALF:HEAD_DIM]
    grad_kv = jnp.concatenate(
        [u * cos + w * sin, w * cos - u * sin, grad_kv[:, HEAD_DIM:]], axis=1
    ).astype(BF)

    query_shard = sum_at_owner(weight_pieces(n1_1, grad_query), ORDERS[1])
    kv_shard = sum_at_owner(weight_pieces(n1_0, grad_kv), ORDERS[0])
    dn1_term = jnp.einsum(
        "rq,dq->rd", grad_query, query_projection_weight, preferred_element_type=F32
    )
    kv_weight = jnp.concatenate([key_projection_weight, value_projection_weight], axis=1)
    dn1_term = dn1_term + jnp.einsum("rq,dq->rd", grad_kv, kv_weight, preferred_element_type=F32)
    grad_gain_attn = jnp.sum(dn1_term * x_all * inverse_attn, axis=0)
    dn1_term = dn1_term.astype(BF)
    dn1 = own_half(dn1_term).astype(F32) + other_core(other_half(dn1_term)).astype(F32)
    x_own = tokens.astype(F32).reshape(block, width)
    inverse_own = lax.rsqrt(jnp.mean(x_own * x_own, axis=-1, keepdims=True) + EPS)
    grad_tokens = own_half(grad_hidden) + rms_backward(x_own, inverse_own, gain_attn, dn1)
    grad_tokens = grad_tokens.astype(BF).reshape(tokens.shape)

    first = tp == 0

    def both_cores(vector):
        none = jnp.zeros_like(vector)
        return jnp.concatenate([jnp.where(first, vector, none), jnp.where(first, none, vector)])

    kv_sums = jnp.sum(grad_kv.astype(F32), axis=0)
    vectors = (
        grad_gain_attn,
        jnp.where(first, grad_gain_mlp, 0.0),
        both_cores(jnp.sum(grad_query.astype(F32), axis=0)),
        both_cores(kv_sums[:HEAD_DIM]),
        both_cores(kv_sums[HEAD_DIM:]),
    )
    sizes = [v.shape[0] for v in vectors]
    packed = jnp.concatenate(vectors).reshape(-1, 128)
    sums = jnp.split(sum_everywhere(packed).reshape(-1), [sum(sizes[:k]) for k in range(1, 5)])
    return (
        mixed,
        grad_tokens,
        sums[0],
        query_shard,
        sums[2],
        kv_shard[:, :HEAD_DIM],
        sums[3],
        kv_shard[:, HEAD_DIM:],
        sums[4],
        output_shard,
        sums[1],
        gate_shard,
        up_shard,
        down_shard,
    )


def solution(mesh):
    split = Mesh(mesh.devices.reshape(SIDE, SIDE, SIDE, mesh.shape["tp"]), (*CTX, "tp"))
    return jax.shard_map(
        local,
        mesh=split,
        in_specs=(
            P(CTX, None, "tp", None),
            P(),
            P(None, "tp"),
            P("tp"),
            P(None, "tp"),
            P("tp"),
            P(None, "tp"),
            P("tp"),
            P("tp", None),
            P(),
            P(None, "tp"),
            P(None, "tp"),
            P("tp", None),
            P(CTX, None, "tp", None),
        ),
        out_specs=(
            P(CTX, None, "tp", None),
            P(CTX, None, "tp", None),
            P(),
            P(CTX, "tp"),
            P(),
            P(CTX, "tp"),
            P(),
            P(CTX, "tp"),
            P(),
            P("tp", CTX),
            P(),
            P(CTX, "tp"),
            P(CTX, "tp"),
            P("tp", CTX),
        ),
        check_vma=False,
    )
```

```python
import functools
import itertools

import jax
import jax.numpy as jnp
from jax import lax
from jax.experimental import pallas as pl
from jax.experimental.pallas import tpu as pltpu
from jax.sharding import Mesh
from jax.sharding import PartitionSpec as P

HEAD_DIM = 64
HEADS = 7
HALF = HEAD_DIM // 2
WIDE = 2 * HEAD_DIM
LANES = 640
CHUNK = 4
CTX = ("ctx_0", "ctx_1", "ctx_2")
ALL = (*CTX, "tp")
NEAR = ("ctx_0", "ctx_1")
FAR = ("ctx_1", "ctx_0")
DEEP = ("ctx_2", "ctx_2")
SIDE = 4
EPS = 1e-06
THETA = 1000000.0
NEG_FILL = -1e30
BF = jnp.bfloat16
F32 = jnp.float32


def columns_of(rows, group, block):
    parts = [
        rows[group * block : (group + 1) * block, h * HEAD_DIM : (h + 1) * HEAD_DIM]
        for h in range(HEADS)
    ]
    parts.append(jnp.zeros((LANES - HEADS * block, HEAD_DIM), rows.dtype))
    return jnp.concatenate(parts, axis=0)


def rows_of(columns, block):
    return jnp.concatenate(
        [columns[h * block : (h + 1) * block] for h in range(HEADS)], axis=1
    )


def slot_of(j, me_ref):
    s0 = (j // SIDE - me_ref[0]) & (SIDE - 1)
    s1 = (j % SIDE - me_ref[1]) & (SIDE - 1)
    return jnp.where(me_ref[3] == 0, s0 * SIDE + s1, s1 * SIDE + s0)


def causal(me2, late, block, query_row):
    shape = (CHUNK, block, LANES)
    b = lax.broadcasted_iota(jnp.int32, shape, 0).reshape(CHUNK * block, LANES)
    r = lax.broadcasted_iota(jnp.int32, shape, 1).reshape(CHUNK * block, LANES)
    ahead = (((b + me2) & (CHUNK - 1)) - me2) * block
    ahead = -ahead if late else ahead
    return ahead + r <= query_row


def forward_step(qt, kv, allowed, carry):
    top, acc = carry
    s = jnp.dot(kv, qt, preferred_element_type=F32)
    if allowed is not None:
        s = jnp.where(allowed, s, NEG_FILL)
    new = jnp.maximum(top, jnp.max(s, axis=0, keepdims=True))
    p = jnp.exp(s - new).astype(BF)
    shrink = jnp.exp(top - new)
    lane = lax.broadcasted_iota(jnp.int32, kv.shape, 1)
    ones_v = jnp.where(lane < HEAD_DIM, BF(1), kv)
    more = lax.dot_general(ones_v, p, (((0,), (0,)), ((), ())), preferred_element_type=F32)
    return new, acc * shrink + more


def no_keys_yet():
    return jnp.full((1, LANES), NEG_FILL, F32), jnp.zeros((WIDE, LANES), F32)


def first_kernel(q_ref, early_ref, cos_ref, sin_ref, qt_ref, top_ref, acc_ref):
    block = q_ref.shape[0] // 2
    for g in (0, 1):
        qt = columns_of(q_ref[...], g, block).T
        u, w = qt[:HALF], qt[HALF:]
        cos, sin = cos_ref[g], sin_ref[g]
        turned = jnp.concatenate([u * cos - w * sin, w * cos + u * sin], axis=0)
        qt_ref[g, :HEAD_DIM] = turned.astype(BF) * BF(0.125)
        qt_ref[g, HEAD_DIM:] = jnp.zeros((HEAD_DIM, LANES), BF)

    def step(slot, carry):
        return forward_step(qt_ref[1], early_ref[slot].reshape(-1, WIDE), None, carry)

    top_ref[...], acc_ref[...] = lax.fori_loop(
        0, early_ref.shape[0], step, no_keys_yet(), unroll=4
    )


def second_kernel(
    me_ref,
    qt_ref,
    top_ref,
    acc_ref,
    early_ref,
    late_ref,
    row_ref,
    ot_ref,
    lse_ref,
    att_ref,
    tops_ref,
    accs_ref,
):
    block = early_ref.shape[2]
    mine = me_ref[0] * SIDE + me_ref[1]
    tops_ref[0], accs_ref[0] = no_keys_yet()
    tops_ref[1], accs_ref[1] = top_ref[...], acc_ref[...]

    def step(i, unused):
        late = i >= mine
        g = late.astype(jnp.int32)
        slot = slot_of(jnp.where(late, i + 1, i), me_ref)
        kv = jnp.where(late, late_ref[slot], early_ref[slot]).reshape(-1, WIDE)
        tops_ref[g], accs_ref[g] = forward_step(
            qt_ref[g], kv, None, (tops_ref[g], accs_ref[g])
        )
        return unused

    lax.fori_loop(0, early_ref.shape[0] - 1, step, 0, unroll=5)
    for g, ref in enumerate((early_ref, late_ref)):
        allowed = causal(me_ref[2], g == 1, block, row_ref[...])
        carry = (tops_ref[g], accs_ref[g])
        top, acc = forward_step(qt_ref[g], ref[0].reshape(-1, WIDE), allowed, carry)
        total = acc[0:1]
        out = acc[HEAD_DIM:] / total
        ot_ref[g] = out
        lse_ref[g] = top + jnp.log(total)
        att_ref[g * block : (g + 1) * block] = rows_of(out.T, block).astype(BF)


def backward_operands(g, qt_ref, ot_ref, lse_ref, grad_ref):
    block = grad_ref.shape[0] // 2
    qt = qt_ref[g]
    grad = columns_of(grad_ref[...].astype(F32), g, block)
    none = jnp.zeros((LANES, HEAD_DIM), F32)
    grad_rows = jnp.concatenate([none, grad], axis=1)
    grad_t = grad_rows.T
    delta = jnp.sum(grad_t[HEAD_DIM:] * ot_ref[g], axis=0, keepdims=True)
    q_rows = qt.astype(F32).T.astype(BF)
    return qt, q_rows, grad_t.astype(BF), grad_rows.astype(BF), lse_ref[g], delta


def backward_step(operands, kv, allowed):
    qt, q_rows, grad_t, grad_rows, lse, delta = operands
    s = jnp.dot(kv, qt, preferred_element_type=F32)
    p = jnp.exp(s - lse)
    if allowed is not None:
        p = jnp.where(allowed, p, 0.0)
    dp = jnp.dot(kv, grad_t, preferred_element_type=F32)
    ds = (p * (dp - delta)).astype(BF)
    dkv = jnp.dot(ds, q_rows, preferred_element_type=F32) + jnp.dot(
        p.astype(BF), grad_rows, preferred_element_type=F32
    )
    dqt = lax.dot_general(kv, ds, (((0,), (0,)), ((), ())), preferred_element_type=F32)
    return dkv, dqt


def back_first_kernel(qt_ref, ot_ref, lse_ref, grad_ref, early_ref, dqt_ref, sum_ref):
    keys = CHUNK * early_ref.shape[2]
    operands = backward_operands(1, qt_ref, ot_ref, lse_ref, grad_ref)

    def step(slot, dqt):
        dkv, more = backward_step(operands, early_ref[slot].reshape(keys, WIDE), None)
        sum_ref[slot] = dkv.reshape(sum_ref.shape[1:])
        return dqt + more

    start = jnp.zeros((WIDE, LANES), F32)
    dqt_ref[...] = lax.fori_loop(0, early_ref.shape[0], step, start, unroll=4)


def back_second_kernel(
    me_ref,
    qt_ref,
    ot_ref,
    lse_ref,
    grad_ref,
    early_ref,
    late_ref,
    cos_ref,
    sin_ref,
    row_ref,
    dqt_ref,
    sum_ref,
    *rest,
):
    scratch, rest = rest[-6:], rest[:-6]
    dq_ref, out_refs = rest[-1 - SIDE], rest[-SIDE:]
    q_rows_ref, grad_t_ref, grad_rows_ref, delta_ref, dqts_ref, dkv_ref = scratch
    block = grad_ref.shape[0] // 2
    keys = CHUNK * block
    mine = me_ref[0] * SIDE + me_ref[1]
    for g in (0, 1):
        unused, q_rows, grad_t, grad_rows, unused, delta = backward_operands(
            g, qt_ref, ot_ref, lse_ref, grad_ref
        )
        q_rows_ref[g], grad_t_ref[g], grad_rows_ref[g] = q_rows, grad_t, grad_rows
        delta_ref[g] = delta

    def operands(g):
        return (
            qt_ref[g],
            q_rows_ref[g],
            grad_t_ref[g],
            grad_rows_ref[g],
            lse_ref[g],
            delta_ref[g],
        )

    def put(slot, part, dkv):
        dkv_ref[slot, :, part] = dkv.reshape(CHUNK, block, WIDE).astype(BF)

    dqts_ref[0] = jnp.zeros((WIDE, LANES), F32)
    dqts_ref[1] = dqt_ref[...]

    def step(i, unused):
        late = i >= mine
        g = late.astype(jnp.int32)
        slot = slot_of(jnp.where(late, i + 1, i), me_ref)
        kv = jnp.where(late, late_ref[slot], early_ref[slot]).reshape(keys, WIDE)
        dkv, more = backward_step(operands(g), kv, None)
        put(slot, 0, sum_ref[slot].reshape(keys, WIDE) + jnp.where(late, 0.0, dkv))
        put(slot, 1, jnp.where(late, dkv, 0.0))
        dqts_ref[g] += more
        return unused

    lax.fori_loop(0, early_ref.shape[0] - 1, step, 0, unroll=5)
    for g, ref in enumerate((early_ref, late_ref)):
        allowed = causal(me_ref[2], g == 1, block, row_ref[...])
        dkv, more = backward_step(operands(g), ref[0].reshape(keys, WIDE), allowed)
        put(0, g, dkv + sum_ref[0].reshape(keys, WIDE) if g == 0 else dkv)
        dqt = dqts_ref[g] + more
        u, w = dqt[:HALF] * 0.125, dqt[HALF:HEAD_DIM] * 0.125
        cos, sin = cos_ref[g], sin_ref[g]
        dq = jnp.concatenate([u * cos + w * sin, w * cos - u * sin], axis=0).T
        dq_ref[g * block : (g + 1) * block] = rows_of(dq, block).astype(dq_ref.dtype)
    for k, out_ref in enumerate(out_refs):
        out_ref[...] = dkv_ref[k * SIDE : (k + 1) * SIDE]


VMEM = pl.BlockSpec(memory_space=pltpu.VMEM)
SMEM = pl.BlockSpec(memory_space=pltpu.SMEM)
PARAMS = pltpu.CompilerParams(vmem_limit_bytes=28 * 1024 * 1024)


def attend_first(q, early, cos, sin):
    return pl.pallas_call(
        first_kernel,
        out_shape=(
            jax.ShapeDtypeStruct((2, WIDE, LANES), BF),
            jax.ShapeDtypeStruct((1, LANES), F32),
            jax.ShapeDtypeStruct((WIDE, LANES), F32),
        ),
        in_specs=[VMEM] * 4,
        out_specs=(VMEM,) * 3,
        compiler_params=PARAMS,
        cost_estimate=pl.CostEstimate(
            flops=13_000_000_000, bytes_accessed=2_000_000, transcendentals=0
        ),
        name="attend_first",
    )(q, early, cos, sin)


def attend_second(me, qt, top, acc, early, late, rows):
    own = 2 * early.shape[2]
    return pl.pallas_call(
        second_kernel,
        out_shape=(
            jax.ShapeDtypeStruct((2, HEAD_DIM, LANES), F32),
            jax.ShapeDtypeStruct((2, 1, LANES), F32),
            jax.ShapeDtypeStruct((own, HEADS * HEAD_DIM), BF),
        ),
        in_specs=[SMEM] + [VMEM] * 6,
        out_specs=(VMEM,) * 3,
        scratch_shapes=[pltpu.VMEM((2, 1, LANES), F32), pltpu.VMEM((2, WIDE, LANES), F32)],
        compiler_params=PARAMS,
        cost_estimate=pl.CostEstimate(
            flops=13_000_000_000, bytes_accessed=2_000_000, transcendentals=0
        ),
        name="attend_second",
    )(me, qt, top, acc, early, late, rows)


def attend_back_first(qt, ot, lse, grad, early):
    return pl.pallas_call(
        back_first_kernel,
        out_shape=(
            jax.ShapeDtypeStruct((WIDE, LANES), F32),
            jax.ShapeDtypeStruct(early.shape, F32),
        ),
        in_specs=[VMEM] * 5,
        out_specs=(VMEM,) * 2,
        compiler_params=PARAMS,
        cost_estimate=pl.CostEstimate(
            flops=14_000_000_000, bytes_accessed=4_000_000, transcendentals=0
        ),
        name="attend_back_first",
    )(qt, ot, lse, grad, early)


def attend_back_second(me, qt, ot, lse, grad, early, late, cos, sin, rows, dqt, sums, before):
    own = grad.shape[0]
    part = (SIDE, CHUNK, 2, *early.shape[2:])
    return pl.pallas_call(
        back_second_kernel,
        out_shape=(
            jax.ShapeDtypeStruct((own, HEADS * HEAD_DIM), BF),
            *[jax.ShapeDtypeStruct(part, BF)] * SIDE,
        ),
        in_specs=[SMEM] + [VMEM] * 11 + [pl.BlockSpec(memory_space=pl.ANY)] * len(before),
        out_specs=(VMEM,) * (1 + SIDE),
        scratch_shapes=[
            pltpu.VMEM((2, LANES, WIDE), BF),
            pltpu.VMEM((2, WIDE, LANES), BF),
            pltpu.VMEM((2, LANES, WIDE), BF),
            pltpu.VMEM((2, 1, LANES), F32),
            pltpu.VMEM((2, WIDE, LANES), F32),
            pltpu.VMEM((SIDE * part[0], *part[1:]), BF),
        ],
        compiler_params=PARAMS,
        cost_estimate=pl.CostEstimate(
            flops=14_000_000_000, bytes_accessed=8_000_000, transcendentals=0
        ),
        name="attend_back_second",
    )(me, qt, ot, lse, grad, early, late, cos, sin, rows, dqt, sums, *before)


def send(array, axes, s):
    pairs = []
    for source in itertools.product(range(SIDE), range(SIDE), range(SIDE), range(2)):
        target = list(source)
        k = CTX.index(axes[source[3]])
        target[k] = (target[k] + s) % SIDE
        pairs.append((linear(source), linear(target)))
    return lax.ppermute(array, ALL, pairs)


def linear(place):
    return ((place[0] * SIDE + place[1]) * SIDE + place[2]) * 2 + place[3]


def fetch(array, axes, s):
    return send(array, axes, SIDE - s)


def other_core(array):
    return lax.ppermute(array, "tp", [(0, 1), (1, 0)])


def gather(array, axes, dim):
    return jnp.stack([array] + [fetch(array, axes, s) for s in range(1, SIDE)], axis=dim)


def total_of(arrays):
    total = arrays[0].astype(F32)
    for a in arrays[1:]:
        total = total + a.astype(F32)
    return total


def sum_level(pieces, axes):
    return total_of([pieces[0]] + [send(pieces[s], axes, s) for s in range(1, SIDE)])


def split(array):
    rows = array.shape[0] // SIDE
    return [array[s * rows : (s + 1) * rows] for s in range(SIDE)]


def swap_and_sum(blocks, axes):
    return jnp.sum(lax.all_to_all(blocks, axes, 0, 0, tiled=True).astype(F32), axis=0)


def by_distance(me, levels, width):
    each = width // SIDE**3
    place = jnp.arange(width)
    part, within = place // each, place % each
    parts = jnp.stack([part // SIDE**2, part // SIDE % SIDE, part % SIDE])
    d0, d1, d2 = [(me[k] + parts[levels[k]]) % SIDE for k in range(3)]
    feature = ((d0 * SIDE + d1) * SIDE + d2) * each + within
    return (jnp.arange(width)[:, None] == feature[None, :]).astype(BF)


def rearranged(rows, table):
    return jnp.dot(rows, table, preferred_element_type=F32).astype(BF)


def weight_grad(rows, grads):
    return lax.dot_general(rows, grads, (((0,), (0,)), ((), ())), preferred_element_type=F32)


def columns(rows):
    size = rows.shape[1] // SIDE
    return [rows[:, s * size : (s + 1) * size] for s in range(SIDE)]


class Ring:
    def __init__(self, rows, grads, axes):
        self.axes, self.grads = axes, grads
        self.rows = columns(rows)
        half = self.rows[0].shape[1] // 2
        self.far = weight_grad(self.rows[2], grads).astype(BF)
        self.between = [
            send(self.far[:half], axes, 1),
            send(self.far[half:], axes, SIDE - 1),
        ]

    def second(self, beside=None):
        none = jnp.zeros(self.between[0].shape, F32)
        right = weight_grad(self.rows[1], self.grads) + jnp.concatenate(
            [self.between[0].astype(F32), none], axis=0
        )
        left = weight_grad(self.rows[3], self.grads) + jnp.concatenate(
            [none, self.between[1].astype(F32)], axis=0
        )
        right, left = right.astype(BF), left.astype(BF)
        if beside is not None:
            right = jnp.concatenate([right, beside[1]], axis=1)
            left = jnp.concatenate([left, beside[3]], axis=1)
        self.arrived = [send(right, self.axes, 1), send(left, self.axes, SIDE - 1)]
        return [right, left]

    def total(self):
        width = self.grads.shape[1]
        arrived = [a[:, :width] for a in self.arrived]
        return total_of([weight_grad(self.rows[0], self.grads), *arrived]).astype(BF)


def rms_forward(rows, gain):
    inverse = lax.rsqrt(jnp.mean(rows * rows, axis=-1, keepdims=True) + EPS)
    return (rows * inverse * gain, inverse)


def rms_backward(rows, inverse, gain, grad_out):
    weighted = grad_out * gain
    inner = jnp.mean(rows * weighted, axis=-1, keepdims=True)
    return inverse * weighted - rows * (inverse * inverse * inverse) * inner


def angles(positions):
    freqs = 1.0 / THETA ** (jnp.arange(0, HEAD_DIM, 2).astype(F32) / HEAD_DIM)
    return positions.astype(F32), freqs


def local(
    tokens,
    gain_attn,
    query_projection_weight,
    query_bias_vector,
    key_projection_weight,
    key_bias_vector,
    value_projection_weight,
    value_bias_vector,
    w_output,
    gain_mlp,
    w_gate,
    w_up,
    w_down,
    cotangent,
):
    me = [lax.axis_index(a) for a in CTX]
    tp = lax.axis_index("tp")
    ctx_count = SIDE**3
    ctx = (me[0] * SIDE + me[1]) * SIDE + me[2]
    half = tokens.shape[2]
    block = 2 * half
    width = tokens.shape[3]
    own = 2 * block
    places = jnp.stack([me[0], me[1], me[2], tp]).astype(jnp.int32)

    def both_halves(array):
        mine = array.reshape(2, half, width)
        theirs = other_core(mine)
        halves = [jnp.where(tp == 0, mine, theirs), jnp.where(tp == 0, theirs, mine)]
        return jnp.stack(halves, axis=1).reshape(own, width)

    def own_half(array):
        return lax.dynamic_index_in_dim(
            array.reshape(2, 2, half, width), tp, 1, keepdims=False
        ).reshape(block, width)

    def other_half(array):
        return lax.dynamic_index_in_dim(
            array.reshape(2, 2, half, width), 1 - tp, 1, keepdims=False
        ).reshape(block, width)

    firsts = jnp.stack([ctx * block, (2 * ctx_count - 1 - ctx) * block])
    row = jnp.arange(LANES) % block
    row = jnp.where(jnp.arange(LANES) < HEADS * block, row, 0)
    lane_places, freqs = angles(firsts[:, None] + row[None, :])
    lane_angles = lane_places[:, None, :] * freqs[None, :, None]
    lane_cos, lane_sin = jnp.cos(lane_angles), jnp.sin(lane_angles)
    own_places, freqs = angles((firsts[:, None] + jnp.arange(block)[None, :]).reshape(-1))
    own_angles = own_places[:, None] * freqs[None, :]
    cos, sin = jnp.cos(own_angles), jnp.sin(own_angles)
    query_row = row.astype(jnp.int32)[None, :]

    x_all = lax.all_gather(tokens.reshape(2, half, width), "tp", axis=0)
    x_all = jnp.moveaxis(x_all, 0, 1).reshape(own, width).astype(F32)
    dy_all = both_halves(cotangent)
    n1, inverse_attn = rms_forward(x_all, gain_attn)
    n1 = n1.astype(BF)
    key_pre = jnp.dot(n1, key_projection_weight, preferred_element_type=F32) + key_bias_vector
    value_pre = jnp.dot(n1, value_projection_weight, preferred_element_type=F32) + value_bias_vector
    u, w = key_pre[:, :HALF], key_pre[:, HALF:]
    kv_own = jnp.concatenate([u * cos - w * sin, w * cos + u * sin, value_pre], axis=1)
    kv_own = kv_own.astype(BF).reshape(2, block, WIDE)
    kv_row = gather(kv_own, DEEP, 1)
    shape = (SIDE * SIDE, CHUNK, block, WIDE)
    early_row = gather(kv_row[0], FAR, 0)
    early = gather(early_row, NEAR, 0).reshape(shape)
    late_row = gather(kv_row[1], FAR, 0)
    late_rows = [fetch(late_row, NEAR, 1)]

    query_pre = (
        jnp.dot(n1, query_projection_weight, preferred_element_type=F32) + query_bias_vector
    )
    near_first = by_distance(me, (2 * tp, 2 - 2 * tp, 1), width)
    deep_first = by_distance(me, (2 - tp, 1 + tp, 0), width)
    grad_act = jnp.einsum("rd,fd->rf", dy_all, w_down, preferred_element_type=F32)
    dy_deep = rearranged(dy_all, deep_first)
    n1_deep = rearranged(n1, deep_first)

    early, late_row, grad_act = lax.optimization_barrier((early, late_row, grad_act))
    late_rows += [fetch(late_row, NEAR, s) for s in range(2, SIDE)]
    qt, top, acc = attend_first(query_pre, early, lane_cos, lane_sin)
    top, acc, *late_rows = lax.optimization_barrier((top, acc, *late_rows))
    late = jnp.stack([late_row, *late_rows]).reshape(shape)
    ot, lse, attended = attend_second(places, qt, top, acc, early, late, query_row)
    attn_term = jnp.dot(attended, w_output, preferred_element_type=F32).astype(BF)
    attn_rows = attn_term.astype(F32) + other_core(attn_term).astype(F32)
    hidden = x_all + attn_rows

    n2, inverse_mlp = rms_forward(hidden, gain_mlp)
    n2 = n2.astype(BF)
    gate_rows = jnp.dot(n2, w_gate, preferred_element_type=F32)
    up_rows = jnp.dot(n2, w_up, preferred_element_type=F32)
    sigmoid_gate = jax.nn.sigmoid(gate_rows)
    silu_gate = gate_rows * sigmoid_gate
    activation = (silu_gate * up_rows).astype(BF)
    grad_gate = (
        grad_act * up_rows * sigmoid_gate * (1.0 + gate_rows * (1.0 - sigmoid_gate))
    ).astype(BF)
    grad_up = (grad_act * silu_gate).astype(BF)
    first = tp == 0
    kept = jnp.where(first, grad_gate, grad_up)
    given = other_core(jnp.where(first, grad_up, grad_gate))
    down_ring = Ring(dy_deep, activation, DEEP)
    grad_gate, grad_up, unused = lax.optimization_barrier((grad_gate, grad_up, down_ring.far))
    dn2_term = (
        jnp.einsum("rf,df->rd", grad_gate, w_gate, preferred_element_type=F32)
        + jnp.einsum("rf,df->rd", grad_up, w_up, preferred_element_type=F32)
    ).astype(BF)
    dn2_other = other_core(dn2_term)
    ring = Ring(rearranged(n2, near_first), jnp.concatenate([kept, given], axis=1), NEAR)
    dn2 = dn2_term.astype(F32) + dn2_other.astype(F32)
    grad_hidden = dy_all.astype(F32) + rms_backward(hidden, inverse_mlp, gain_mlp, dn2)
    grad_gain_mlp = jnp.sum(dn2 * hidden * inverse_mlp, axis=0)
    grad_attn = grad_hidden.astype(BF)
    grad_attended = jnp.einsum(
        "rd,qd->rq", grad_attn, w_output, preferred_element_type=F32
    ).astype(BF)
    output_pieces = [
        weight_grad(r, attended).astype(BF) for r in columns(rearranged(grad_attn, deep_first))
    ]

    dqt, sums = attend_back_first(qt, ot, lse, grad_attended, early)
    dqt, *between = lax.optimization_barrier((dqt, *ring.between, *down_ring.between))
    ring.between, down_ring.between = between[:2], between[2:]
    before = [*output_pieces, *down_ring.second(output_pieces), *ring.second()]
    grad_query, *grad_kv = attend_back_second(
        places, qt, ot, lse, grad_attended, early, late, lane_cos, lane_sin, query_row, dqt, sums, before
    )
    grad_query, activation, *held = lax.optimization_barrier(
        (grad_query, activation, *grad_kv, *down_ring.arrived)
    )
    grad_kv, down_ring.arrived = held[:SIDE], held[SIDE:]

    inner = HEADS * HEAD_DIM
    output_far = send(output_pieces[2], DEEP, 2)
    grad_kv = [part.reshape(-1, block, WIDE) for part in grad_kv]
    grad_kv = sum_level(grad_kv, NEAR).astype(BF)
    query_pieces = [weight_grad(r, grad_query).astype(BF) for r in columns(n1_deep)]
    query_near = sum_level(query_pieces, DEEP).astype(BF)
    grad_kv, weights, *unused = lax.optimization_barrier((grad_kv, ring.total(), *query_pieces))
    grad_kv = sum_level(split(grad_kv), FAR).astype(BF)
    weights = sum_level(split(weights), DEEP).astype(BF)
    output_near = [output_pieces[0], output_far] + [a[:, -inner:] for a in down_ring.arrived]
    output_near = total_of(output_near).astype(BF)
    downs = jnp.concatenate([down_ring.total(), output_near, query_near], axis=1)
    grad_kv, downs = lax.optimization_barrier((grad_kv, downs))
    grad_kv = sum_level(split(grad_kv), DEEP)
    downs = sum_level(split(downs), FAR).astype(BF)
    mlp_term = jnp.dot(activation, w_down, preferred_element_type=F32).astype(BF)
    mlp_rows = own_half(mlp_term).astype(F32) + other_core(other_half(mlp_term)).astype(F32)
    mixed = (own_half(hidden) + mlp_rows).astype(BF).reshape(tokens.shape)

    grad_kv, weights, mixed = lax.optimization_barrier((grad_kv, weights, mixed))
    grad_kv = grad_kv.reshape(own, WIDE)
    weights = sum_level(split(weights), FAR)
    downs = sum_level(split(downs), NEAR)
    units = grad_gate.shape[1]
    mine, theirs = weights[:, :units], other_core(weights[:, units:])
    gate_shard, up_shard = jnp.where(first, mine, theirs), jnp.where(first, theirs, mine)
    down_shard = downs[:, :units].T
    output_shard = downs[:, units : units + inner].T
    query_shard = downs[:, units + inner :]

    u, w = grad_kv[:, :HALF], grad_kv[:, HALF:HEAD_DIM]
    grad_kv = jnp.concatenate(
        [u * cos + w * sin, w * cos - u * sin, grad_kv[:, HEAD_DIM:]], axis=1
    ).astype(BF)

    dn1_term = jnp.einsum(
        "rq,dq->rd", grad_query, query_projection_weight, preferred_element_type=F32
    )
    kv_weight = jnp.concatenate([key_projection_weight, value_projection_weight], axis=1)
    dn1_term = dn1_term + jnp.einsum("rq,dq->rd", grad_kv, kv_weight, preferred_element_type=F32)
    grad_gain_attn = jnp.sum(dn1_term * x_all * inverse_attn, axis=0)
    dn1_term = dn1_term.astype(BF)
    dn1 = own_half(dn1_term).astype(F32) + other_core(other_half(dn1_term)).astype(F32)
    x_own = tokens.astype(F32).reshape(block, width)
    inverse_own = lax.rsqrt(jnp.mean(x_own * x_own, axis=-1, keepdims=True) + EPS)
    grad_tokens = own_half(grad_hidden) + rms_backward(x_own, inverse_own, gain_attn, dn1)
    grad_tokens = grad_tokens.astype(BF).reshape(tokens.shape)

    kv_sums = jnp.sum(grad_kv.astype(F32), axis=0)
    kv_high = lax.reduce_precision(kv_sums, 8, 7)
    vectors = (
        grad_gain_attn,
        jnp.where(tp == 0, grad_gain_mlp, 0.0),
        jnp.sum(grad_query.astype(F32), axis=0),
        jnp.zeros((-inner % WIDE,), F32),
        kv_high,
        kv_sums - kv_high,
    )
    packed = jnp.concatenate([v.astype(BF) for v in vectors]).reshape(-1, WIDE)
    owners, lines = SIDE**3, packed.shape[0]
    own_kv = weight_grad(n1, grad_kv).astype(BF).reshape(owners, -1, WIDE)
    each = own_kv.shape[1]
    message = jnp.concatenate(
        [
            own_kv,
            jnp.broadcast_to(packed[None], (owners, *packed.shape)),
            jnp.zeros((owners, -(each + lines) % 8, WIDE), BF),
        ],
        axis=1,
    )
    message = swap_and_sum(message, CTX)
    kv_shard = message[:each]
    packed = message[each : each + lines]
    packed = jnp.concatenate([packed[:-2], packed[-2:-1] + packed[-1:]])
    packed_other = other_core(packed)
    both = packed + packed_other
    gains = both.reshape(-1)[: 2 * width]
    packed, packed_other = packed.reshape(-1)[2 * width :], packed_other.reshape(-1)[2 * width :]
    lower = jnp.where(tp == 0, packed, packed_other)
    upper = jnp.where(tp == 0, packed_other, packed)

    def both_cores(first, last):
        return jnp.concatenate([lower[first:last], upper[first:last]])

    keys_at = packed.shape[0] - WIDE
    return (
        mixed,
        grad_tokens,
        gains[:width],
        query_shard,
        both_cores(0, inner),
        kv_shard[:, :HEAD_DIM],
        both_cores(keys_at, keys_at + HEAD_DIM),
        kv_shard[:, HEAD_DIM:],
        both_cores(keys_at + HEAD_DIM, keys_at + WIDE),
        output_shard,
        gains[width:],
        gate_shard,
        up_shard,
        down_shard,
    )


def solution(mesh):
    split = Mesh(mesh.devices.reshape(SIDE, SIDE, SIDE, mesh.shape["tp"]), (*CTX, "tp"))
    return jax.shard_map(
        local,
        mesh=split,
        in_specs=(
            P(CTX, None, "tp", None),
            P(),
            P(None, "tp"),
            P("tp"),
            P(None, "tp"),
            P("tp"),
            P(None, "tp"),
            P("tp"),
            P("tp", None),
            P(),
            P(None, "tp"),
            P(None, "tp"),
            P("tp", None),
            P(CTX, None, "tp", None),
        ),
        out_specs=(
            P(CTX, None, "tp", None),
            P(CTX, None, "tp", None),
            P(),
            P(CTX, "tp"),
            P(),
            P(CTX, "tp"),
            P(),
            P(CTX, "tp"),
            P(),
            P("tp", CTX),
            P(),
            P(CTX, "tp"),
            P(CTX, "tp"),
            P("tp", CTX),
        ),
        check_vma=False,
    )
```

```python
import functools
import itertools

import jax
import jax.numpy as jnp
from jax import lax
from jax.experimental import pallas as pl
from jax.experimental.pallas import tpu as pltpu
from jax.sharding import Mesh
from jax.sharding import PartitionSpec as P

HEAD_DIM = 64
HEADS = 7
HALF = HEAD_DIM // 2
WIDE = 2 * HEAD_DIM
LANES = 640
CHUNK = 4
CTX = ("ctx_0", "ctx_1", "ctx_2")
ALL = (*CTX, "tp")
NEAR = ("ctx_0", "ctx_1")
FAR = ("ctx_1", "ctx_0")
DEEP = ("ctx_2", "ctx_2")
SIDE = 4
EPS = 1e-06
THETA = 1000000.0
NEG_FILL = -1e30
BF = jnp.bfloat16
F32 = jnp.float32


def columns_of(rows, group, block):
    parts = [
        rows[group * block : (group + 1) * block, h * HEAD_DIM : (h + 1) * HEAD_DIM]
        for h in range(HEADS)
    ]
    parts.append(jnp.zeros((LANES - HEADS * block, HEAD_DIM), rows.dtype))
    return jnp.concatenate(parts, axis=0)


def rows_of(columns, block):
    return jnp.concatenate(
        [columns[h * block : (h + 1) * block] for h in range(HEADS)], axis=1
    )


def slot_of(j, me_ref):
    s0 = (j // SIDE - me_ref[0]) & (SIDE - 1)
    s1 = (j % SIDE - me_ref[1]) & (SIDE - 1)
    return jnp.where(me_ref[3] == 0, s0 * SIDE + s1, s1 * SIDE + s0)


def causal(me2, late, block, query_row):
    shape = (CHUNK, block, LANES)
    b = lax.broadcasted_iota(jnp.int32, shape, 0).reshape(CHUNK * block, LANES)
    r = lax.broadcasted_iota(jnp.int32, shape, 1).reshape(CHUNK * block, LANES)
    ahead = (((b + me2) & (CHUNK - 1)) - me2) * block
    ahead = -ahead if late else ahead
    return ahead + r <= query_row


def forward_step(qt, kv, allowed, carry):
    top, acc = carry
    s = jnp.dot(kv, qt, preferred_element_type=F32)
    if allowed is not None:
        s = jnp.where(allowed, s, NEG_FILL)
    new = jnp.maximum(top, jnp.max(s, axis=0, keepdims=True))
    p = jnp.exp(s - new).astype(BF)
    shrink = jnp.exp(top - new)
    lane = lax.broadcasted_iota(jnp.int32, kv.shape, 1)
    ones_v = jnp.where(lane < HEAD_DIM, BF(1), kv)
    more = lax.dot_general(ones_v, p, (((0,), (0,)), ((), ())), preferred_element_type=F32)
    return new, acc * shrink + more


def no_keys_yet():
    return jnp.full((1, LANES), NEG_FILL, F32), jnp.zeros((WIDE, LANES), F32)


def first_kernel(q_ref, early_ref, cos_ref, sin_ref, qt_ref, top_ref, acc_ref):
    block = q_ref.shape[0] // 2
    for g in (0, 1):
        qt = columns_of(q_ref[...], g, block).T
        u, w = qt[:HALF], qt[HALF:]
        cos, sin = cos_ref[g], sin_ref[g]
        turned = jnp.concatenate([u * cos - w * sin, w * cos + u * sin], axis=0)
        qt_ref[g, :HEAD_DIM] = turned.astype(BF) * BF(0.125)
        qt_ref[g, HEAD_DIM:] = jnp.zeros((HEAD_DIM, LANES), BF)

    def step(slot, carry):
        return forward_step(qt_ref[1], early_ref[slot].reshape(-1, WIDE), None, carry)

    top_ref[...], acc_ref[...] = lax.fori_loop(
        0, early_ref.shape[0], step, no_keys_yet(), unroll=4
    )


def second_kernel(
    me_ref,
    qt_ref,
    top_ref,
    acc_ref,
    early_ref,
    late_ref,
    row_ref,
    ot_ref,
    lse_ref,
    att_ref,
    tops_ref,
    accs_ref,
):
    block = early_ref.shape[2]
    mine = me_ref[0] * SIDE + me_ref[1]
    tops_ref[0], accs_ref[0] = no_keys_yet()
    tops_ref[1], accs_ref[1] = top_ref[...], acc_ref[...]

    def step(i, unused):
        late = i >= mine
        g = late.astype(jnp.int32)
        slot = slot_of(jnp.where(late, i + 1, i), me_ref)
        kv = jnp.where(late, late_ref[slot], early_ref[slot]).reshape(-1, WIDE)
        tops_ref[g], accs_ref[g] = forward_step(
            qt_ref[g], kv, None, (tops_ref[g], accs_ref[g])
        )
        return unused

    lax.fori_loop(0, early_ref.shape[0] - 1, step, 0, unroll=5)
    for g, ref in enumerate((early_ref, late_ref)):
        allowed = causal(me_ref[2], g == 1, block, row_ref[...])
        carry = (tops_ref[g], accs_ref[g])
        top, acc = forward_step(qt_ref[g], ref[0].reshape(-1, WIDE), allowed, carry)
        total = acc[0:1]
        out = acc[HEAD_DIM:] / total
        ot_ref[g] = out
        lse_ref[g] = top + jnp.log(total)
        att_ref[g * block : (g + 1) * block] = rows_of(out.T, block).astype(BF)


def backward_operands(g, qt_ref, ot_ref, lse_ref, grad_ref):
    block = grad_ref.shape[0] // 2
    qt = qt_ref[g]
    grad = columns_of(grad_ref[...].astype(F32), g, block)
    none = jnp.zeros((LANES, HEAD_DIM), F32)
    grad_rows = jnp.concatenate([none, grad], axis=1)
    grad_t = grad_rows.T
    delta = jnp.sum(grad_t[HEAD_DIM:] * ot_ref[g], axis=0, keepdims=True)
    q_rows = qt.astype(F32).T.astype(BF)
    return qt, q_rows, grad_t.astype(BF), grad_rows.astype(BF), lse_ref[g], delta


def backward_step(operands, kv, allowed):
    qt, q_rows, grad_t, grad_rows, lse, delta = operands
    s = jnp.dot(kv, qt, preferred_element_type=F32)
    p = jnp.exp(s - lse)
    if allowed is not None:
        p = jnp.where(allowed, p, 0.0)
    dp = jnp.dot(kv, grad_t, preferred_element_type=F32)
    ds = (p * (dp - delta)).astype(BF)
    dkv = jnp.dot(ds, q_rows, preferred_element_type=F32) + jnp.dot(
        p.astype(BF), grad_rows, preferred_element_type=F32
    )
    dqt = lax.dot_general(kv, ds, (((0,), (0,)), ((), ())), preferred_element_type=F32)
    return dkv, dqt


def back_first_kernel(qt_ref, ot_ref, lse_ref, grad_ref, early_ref, dqt_ref, sum_ref):
    keys = CHUNK * early_ref.shape[2]
    operands = backward_operands(1, qt_ref, ot_ref, lse_ref, grad_ref)

    def step(slot, dqt):
        dkv, more = backward_step(operands, early_ref[slot].reshape(keys, WIDE), None)
        sum_ref[slot] = dkv.reshape(sum_ref.shape[1:])
        return dqt + more

    start = jnp.zeros((WIDE, LANES), F32)
    dqt_ref[...] = lax.fori_loop(0, early_ref.shape[0], step, start, unroll=4)


def back_second_kernel(
    me_ref,
    qt_ref,
    ot_ref,
    lse_ref,
    grad_ref,
    early_ref,
    late_ref,
    cos_ref,
    sin_ref,
    row_ref,
    dqt_ref,
    sum_ref,
    *rest,
):
    scratch, rest = rest[-6:], rest[:-6]
    dq_ref, out_refs = rest[-1 - SIDE], rest[-SIDE:]
    q_rows_ref, grad_t_ref, grad_rows_ref, delta_ref, dqts_ref, dkv_ref = scratch
    block = grad_ref.shape[0] // 2
    keys = CHUNK * block
    mine = me_ref[0] * SIDE + me_ref[1]
    for g in (0, 1):
        unused, q_rows, grad_t, grad_rows, unused, delta = backward_operands(
            g, qt_ref, ot_ref, lse_ref, grad_ref
        )
        q_rows_ref[g], grad_t_ref[g], grad_rows_ref[g] = q_rows, grad_t, grad_rows
        delta_ref[g] = delta

    def operands(g):
        return (
            qt_ref[g],
            q_rows_ref[g],
            grad_t_ref[g],
            grad_rows_ref[g],
            lse_ref[g],
            delta_ref[g],
        )

    def put(slot, part, dkv):
        dkv_ref[slot, :, part] = dkv.reshape(CHUNK, block, WIDE).astype(BF)

    dqts_ref[0] = jnp.zeros((WIDE, LANES), F32)
    dqts_ref[1] = dqt_ref[...]

    def step(i, unused):
        late = i >= mine
        g = late.astype(jnp.int32)
        slot = slot_of(jnp.where(late, i + 1, i), me_ref)
        kv = jnp.where(late, late_ref[slot], early_ref[slot]).reshape(keys, WIDE)
        dkv, more = backward_step(operands(g), kv, None)
        put(slot, 0, sum_ref[slot].reshape(keys, WIDE) + jnp.where(late, 0.0, dkv))
        put(slot, 1, jnp.where(late, dkv, 0.0))
        dqts_ref[g] += more
        return unused

    lax.fori_loop(0, early_ref.shape[0] - 1, step, 0, unroll=5)
    for g, ref in enumerate((early_ref, late_ref)):
        allowed = causal(me_ref[2], g == 1, block, row_ref[...])
        dkv, more = backward_step(operands(g), ref[0].reshape(keys, WIDE), allowed)
        put(0, g, dkv + sum_ref[0].reshape(keys, WIDE) if g == 0 else dkv)
        dqt = dqts_ref[g] + more
        u, w = dqt[:HALF] * 0.125, dqt[HALF:HEAD_DIM] * 0.125
        cos, sin = cos_ref[g], sin_ref[g]
        dq = jnp.concatenate([u * cos + w * sin, w * cos - u * sin], axis=0).T
        dq_ref[g * block : (g + 1) * block] = rows_of(dq, block).astype(dq_ref.dtype)
    for k, out_ref in enumerate(out_refs):
        out_ref[...] = dkv_ref[k * SIDE : (k + 1) * SIDE]


VMEM = pl.BlockSpec(memory_space=pltpu.VMEM)
SMEM = pl.BlockSpec(memory_space=pltpu.SMEM)
PARAMS = pltpu.CompilerParams(vmem_limit_bytes=28 * 1024 * 1024)


def attend_first(q, early, cos, sin):
    return pl.pallas_call(
        first_kernel,
        out_shape=(
            jax.ShapeDtypeStruct((2, WIDE, LANES), BF),
            jax.ShapeDtypeStruct((1, LANES), F32),
            jax.ShapeDtypeStruct((WIDE, LANES), F32),
        ),
        in_specs=[VMEM] * 4,
        out_specs=(VMEM,) * 3,
        compiler_params=PARAMS,
        cost_estimate=pl.CostEstimate(
            flops=13_000_000_000, bytes_accessed=2_000_000, transcendentals=0
        ),
        name="attend_first",
    )(q, early, cos, sin)


def attend_second(me, qt, top, acc, early, late, rows):
    own = 2 * early.shape[2]
    return pl.pallas_call(
        second_kernel,
        out_shape=(
            jax.ShapeDtypeStruct((2, HEAD_DIM, LANES), F32),
            jax.ShapeDtypeStruct((2, 1, LANES), F32),
            jax.ShapeDtypeStruct((own, HEADS * HEAD_DIM), BF),
        ),
        in_specs=[SMEM] + [VMEM] * 6,
        out_specs=(VMEM,) * 3,
        scratch_shapes=[pltpu.VMEM((2, 1, LANES), F32), pltpu.VMEM((2, WIDE, LANES), F32)],
        compiler_params=PARAMS,
        cost_estimate=pl.CostEstimate(
            flops=13_000_000_000, bytes_accessed=2_000_000, transcendentals=0
        ),
        name="attend_second",
    )(me, qt, top, acc, early, late, rows)


def attend_back_first(qt, ot, lse, grad, early):
    return pl.pallas_call(
        back_first_kernel,
        out_shape=(
            jax.ShapeDtypeStruct((WIDE, LANES), F32),
            jax.ShapeDtypeStruct(early.shape, F32),
        ),
        in_specs=[VMEM] * 5,
        out_specs=(VMEM,) * 2,
        compiler_params=PARAMS,
        cost_estimate=pl.CostEstimate(
            flops=14_000_000_000, bytes_accessed=4_000_000, transcendentals=0
        ),
        name="attend_back_first",
    )(qt, ot, lse, grad, early)


def attend_back_second(me, qt, ot, lse, grad, early, late, cos, sin, rows, dqt, sums, before):
    own = grad.shape[0]
    part = (SIDE, CHUNK, 2, *early.shape[2:])
    return pl.pallas_call(
        back_second_kernel,
        out_shape=(
            jax.ShapeDtypeStruct((own, HEADS * HEAD_DIM), BF),
            *[jax.ShapeDtypeStruct(part, BF)] * SIDE,
        ),
        in_specs=[SMEM] + [VMEM] * 11 + [pl.BlockSpec(memory_space=pl.ANY)] * len(before),
        out_specs=(VMEM,) * (1 + SIDE),
        scratch_shapes=[
            pltpu.VMEM((2, LANES, WIDE), BF),
            pltpu.VMEM((2, WIDE, LANES), BF),
            pltpu.VMEM((2, LANES, WIDE), BF),
            pltpu.VMEM((2, 1, LANES), F32),
            pltpu.VMEM((2, WIDE, LANES), F32),
            pltpu.VMEM((SIDE * part[0], *part[1:]), BF),
        ],
        compiler_params=PARAMS,
        cost_estimate=pl.CostEstimate(
            flops=14_000_000_000, bytes_accessed=8_000_000, transcendentals=0
        ),
        name="attend_back_second",
    )(me, qt, ot, lse, grad, early, late, cos, sin, rows, dqt, sums, *before)


def send(array, axes, s):
    pairs = []
    for source in itertools.product(range(SIDE), range(SIDE), range(SIDE), range(2)):
        target = list(source)
        k = CTX.index(axes[source[3]])
        target[k] = (target[k] + s) % SIDE
        pairs.append((linear(source), linear(target)))
    return lax.ppermute(array, ALL, pairs)


def linear(place):
    return ((place[0] * SIDE + place[1]) * SIDE + place[2]) * 2 + place[3]


def fetch(array, axes, s):
    return send(array, axes, SIDE - s)


def other_core(array):
    return lax.ppermute(array, "tp", [(0, 1), (1, 0)])


def gather(array, axes, dim):
    return jnp.stack([array] + [fetch(array, axes, s) for s in range(1, SIDE)], axis=dim)


def total_of(arrays):
    total = arrays[0].astype(F32)
    for a in arrays[1:]:
        total = total + a.astype(F32)
    return total


def sum_level(pieces, axes):
    return total_of([pieces[0]] + [send(pieces[s], axes, s) for s in range(1, SIDE)])


def split(array):
    rows = array.shape[0] // SIDE
    return [array[s * rows : (s + 1) * rows] for s in range(SIDE)]


def swap_and_sum(blocks, axes):
    return jnp.sum(lax.all_to_all(blocks, axes, 0, 0, tiled=True).astype(F32), axis=0)


def by_distance(me, levels, width):
    each = width // SIDE**3
    place = jnp.arange(width)
    part, within = place // each, place % each
    parts = jnp.stack([part // SIDE**2, part // SIDE % SIDE, part % SIDE])
    d0, d1, d2 = [(me[k] + parts[levels[k]]) % SIDE for k in range(3)]
    feature = ((d0 * SIDE + d1) * SIDE + d2) * each + within
    return (jnp.arange(width)[:, None] == feature[None, :]).astype(BF)


def rearranged(rows, table):
    return jnp.dot(rows, table, preferred_element_type=F32).astype(BF)


def weight_grad(rows, grads):
    return lax.dot_general(rows, grads, (((0,), (0,)), ((), ())), preferred_element_type=F32)


def columns(rows):
    size = rows.shape[1] // SIDE
    return [rows[:, s * size : (s + 1) * size] for s in range(SIDE)]


class Ring:
    def __init__(self, rows, grads, axes):
        self.axes, self.grads = axes, grads
        self.rows = columns(rows)
        half = self.rows[0].shape[1] // 2
        self.far = weight_grad(self.rows[2], grads).astype(BF)
        self.between = [
            send(self.far[:half], axes, 1),
            send(self.far[half:], axes, SIDE - 1),
        ]

    def second(self, beside=None):
        none = jnp.zeros(self.between[0].shape, F32)
        right = weight_grad(self.rows[1], self.grads) + jnp.concatenate(
            [self.between[0].astype(F32), none], axis=0
        )
        left = weight_grad(self.rows[3], self.grads) + jnp.concatenate(
            [none, self.between[1].astype(F32)], axis=0
        )
        right, left = right.astype(BF), left.astype(BF)
        if beside is not None:
            right = jnp.concatenate([right, beside[1]], axis=1)
            left = jnp.concatenate([left, beside[3]], axis=1)
        self.arrived = [send(right, self.axes, 1), send(left, self.axes, SIDE - 1)]
        return [right, left]

    def total(self):
        width = self.grads.shape[1]
        arrived = [a[:, :width] for a in self.arrived]
        return total_of([weight_grad(self.rows[0], self.grads), *arrived]).astype(BF)


def rms_forward(rows, gain):
    inverse = lax.rsqrt(jnp.mean(rows * rows, axis=-1, keepdims=True) + EPS)
    return (rows * inverse * gain, inverse)


def rms_backward(rows, inverse, gain, grad_out):
    weighted = grad_out * gain
    inner = jnp.mean(rows * weighted, axis=-1, keepdims=True)
    return inverse * weighted - rows * (inverse * inverse * inverse) * inner


def angles(positions):
    freqs = 1.0 / THETA ** (jnp.arange(0, HEAD_DIM, 2).astype(F32) / HEAD_DIM)
    return positions.astype(F32), freqs


def local(
    tokens,
    gain_attn,
    query_projection_weight,
    query_bias_vector,
    key_projection_weight,
    key_bias_vector,
    value_projection_weight,
    value_bias_vector,
    w_output,
    gain_mlp,
    w_gate,
    w_up,
    w_down,
    cotangent,
):
    me = [lax.axis_index(a) for a in CTX]
    tp = lax.axis_index("tp")
    ctx_count = SIDE**3
    ctx = (me[0] * SIDE + me[1]) * SIDE + me[2]
    half = tokens.shape[2]
    block = 2 * half
    width = tokens.shape[3]
    own = 2 * block
    places = jnp.stack([me[0], me[1], me[2], tp]).astype(jnp.int32)

    def both_halves(array):
        mine = array.reshape(2, half, width)
        theirs = other_core(mine)
        halves = [jnp.where(tp == 0, mine, theirs), jnp.where(tp == 0, theirs, mine)]
        return jnp.stack(halves, axis=1).reshape(own, width)

    def own_half(array):
        return lax.dynamic_index_in_dim(
            array.reshape(2, 2, half, width), tp, 1, keepdims=False
        ).reshape(block, width)

    def other_half(array):
        return lax.dynamic_index_in_dim(
            array.reshape(2, 2, half, width), 1 - tp, 1, keepdims=False
        ).reshape(block, width)

    firsts = jnp.stack([ctx * block, (2 * ctx_count - 1 - ctx) * block])
    row = jnp.arange(LANES) % block
    row = jnp.where(jnp.arange(LANES) < HEADS * block, row, 0)
    lane_places, freqs = angles(firsts[:, None] + row[None, :])
    lane_angles = lane_places[:, None, :] * freqs[None, :, None]
    lane_cos, lane_sin = jnp.cos(lane_angles), jnp.sin(lane_angles)
    own_places, freqs = angles((firsts[:, None] + jnp.arange(block)[None, :]).reshape(-1))
    own_angles = own_places[:, None] * freqs[None, :]
    cos, sin = jnp.cos(own_angles), jnp.sin(own_angles)
    query_row = row.astype(jnp.int32)[None, :]

    x_all = lax.all_gather(tokens.reshape(2, half, width), "tp", axis=0)
    x_all = jnp.moveaxis(x_all, 0, 1).reshape(own, width).astype(F32)
    dy_all = both_halves(cotangent)
    n1, inverse_attn = rms_forward(x_all, gain_attn)
    n1 = n1.astype(BF)
    key_pre = jnp.dot(n1, key_projection_weight, preferred_element_type=F32) + key_bias_vector
    value_pre = jnp.dot(n1, value_projection_weight, preferred_element_type=F32) + value_bias_vector
    u, w = key_pre[:, :HALF], key_pre[:, HALF:]
    kv_own = jnp.concatenate([u * cos - w * sin, w * cos + u * sin, value_pre], axis=1)
    kv_own = kv_own.astype(BF).reshape(2, block, WIDE)
    kv_row = gather(kv_own, DEEP, 1)
    shape = (SIDE * SIDE, CHUNK, block, WIDE)
    early_row = gather(kv_row[0], FAR, 0)
    early = gather(early_row, NEAR, 0).reshape(shape)
    late_row = gather(kv_row[1], FAR, 0)
    late_rows = [fetch(late_row, NEAR, 1)]

    query_pre = (
        jnp.dot(n1, query_projection_weight, preferred_element_type=F32) + query_bias_vector
    )
    near_first = by_distance(me, (tp, 1 - tp, 2), width)
    deep_first = by_distance(me, (2 - tp, 1 + tp, 0), width)
    grad_act = jnp.einsum("rd,fd->rf", dy_all, w_down, preferred_element_type=F32)
    dy_deep = rearranged(dy_all, deep_first)
    n1_deep = rearranged(n1, deep_first)

    early, late_row, grad_act = lax.optimization_barrier((early, late_row, grad_act))
    late_rows += [fetch(late_row, NEAR, s) for s in range(2, SIDE)]
    qt, top, acc = attend_first(query_pre, early, lane_cos, lane_sin)
    top, acc, *late_rows = lax.optimization_barrier((top, acc, *late_rows))
    late = jnp.stack([late_row, *late_rows]).reshape(shape)
    ot, lse, attended = attend_second(places, qt, top, acc, early, late, query_row)
    attn_term = jnp.dot(attended, w_output, preferred_element_type=F32).astype(BF)
    attn_rows = attn_term.astype(F32) + other_core(attn_term).astype(F32)
    hidden = x_all + attn_rows

    n2, inverse_mlp = rms_forward(hidden, gain_mlp)
    n2 = n2.astype(BF)
    gate_rows = jnp.dot(n2, w_gate, preferred_element_type=F32)
    up_rows = jnp.dot(n2, w_up, preferred_element_type=F32)
    sigmoid_gate = jax.nn.sigmoid(gate_rows)
    silu_gate = gate_rows * sigmoid_gate
    activation = (silu_gate * up_rows).astype(BF)
    grad_gate = (
        grad_act * up_rows * sigmoid_gate * (1.0 + gate_rows * (1.0 - sigmoid_gate))
    ).astype(BF)
    grad_up = (grad_act * silu_gate).astype(BF)
    first = tp == 0
    kept = jnp.where(first, grad_gate, grad_up)
    given = other_core(jnp.where(first, grad_up, grad_gate))
    down_ring = Ring(dy_deep, activation, DEEP)
    grad_gate, grad_up, unused = lax.optimization_barrier((grad_gate, grad_up, down_ring.far))
    dn2_term = (
        jnp.einsum("rf,df->rd", grad_gate, w_gate, preferred_element_type=F32)
        + jnp.einsum("rf,df->rd", grad_up, w_up, preferred_element_type=F32)
    ).astype(BF)
    dn2_other = other_core(dn2_term)
    ring = Ring(rearranged(n2, near_first), jnp.concatenate([kept, given], axis=1), NEAR)
    dn2 = dn2_term.astype(F32) + dn2_other.astype(F32)
    grad_hidden = dy_all.astype(F32) + rms_backward(hidden, inverse_mlp, gain_mlp, dn2)
    grad_gain_mlp = jnp.sum(dn2 * hidden * inverse_mlp, axis=0)
    grad_attn = grad_hidden.astype(BF)
    grad_attended = jnp.einsum(
        "rd,qd->rq", grad_attn, w_output, preferred_element_type=F32
    ).astype(BF)
    output_pieces = [
        weight_grad(r, attended).astype(BF) for r in columns(rearranged(grad_attn, deep_first))
    ]

    dqt, sums = attend_back_first(qt, ot, lse, grad_attended, early)
    dqt, *between = lax.optimization_barrier((dqt, *ring.between, *down_ring.between))
    ring.between, down_ring.between = between[:2], between[2:]
    before = [*output_pieces, *down_ring.second(output_pieces), *ring.second()]
    grad_query, *grad_kv = attend_back_second(
        places, qt, ot, lse, grad_attended, early, late, lane_cos, lane_sin, query_row, dqt, sums, before
    )
    grad_query, activation, *held = lax.optimization_barrier(
        (grad_query, activation, *grad_kv, *down_ring.arrived)
    )
    grad_kv, down_ring.arrived = held[:SIDE], held[SIDE:]

    inner = HEADS * HEAD_DIM
    output_far = send(output_pieces[2], DEEP, 2)
    grad_kv = [part.reshape(-1, block, WIDE) for part in grad_kv]
    grad_kv = sum_level(grad_kv, NEAR).astype(BF)
    query_pieces = [weight_grad(r, grad_query).astype(BF) for r in columns(n1_deep)]
    grad_kv, *held = lax.optimization_barrier((grad_kv, *ring.arrived, *query_pieces))
    ring.arrived, query_pieces = held[:2], held[2:]
    grad_kv = sum_level(split(grad_kv), FAR).astype(BF)
    query_near = sum_level(query_pieces, DEEP).astype(BF)
    output_near = [output_pieces[0], output_far] + [a[:, -inner:] for a in down_ring.arrived]
    output_near = total_of(output_near).astype(BF)
    downs = jnp.concatenate([down_ring.total(), output_near, query_near], axis=1)
    grad_kv, weights = lax.optimization_barrier((grad_kv, ring.total()))
    grad_kv = sum_level(split(grad_kv), DEEP)
    mlp_term = jnp.dot(activation, w_down, preferred_element_type=F32).astype(BF)
    mlp_rows = own_half(mlp_term).astype(F32) + other_core(other_half(mlp_term)).astype(F32)
    mixed = (own_half(hidden) + mlp_rows).astype(BF).reshape(tokens.shape)

    weights = sum_level(split(weights), FAR).astype(BF)
    grad_kv, mixed = lax.optimization_barrier((grad_kv, mixed))
    grad_kv = grad_kv.reshape(own, WIDE)
    u, w = grad_kv[:, :HALF], grad_kv[:, HALF:HEAD_DIM]
    grad_kv = jnp.concatenate(
        [u * cos + w * sin, w * cos - u * sin, grad_kv[:, HEAD_DIM:]], axis=1
    ).astype(BF)

    dn1_term = jnp.einsum(
        "rq,dq->rd", grad_query, query_projection_weight, preferred_element_type=F32
    )
    kv_weight = jnp.concatenate([key_projection_weight, value_projection_weight], axis=1)
    dn1_term = dn1_term + jnp.einsum("rq,dq->rd", grad_kv, kv_weight, preferred_element_type=F32)
    grad_gain_attn = jnp.sum(dn1_term * x_all * inverse_attn, axis=0)
    dn1_term = dn1_term.astype(BF)
    dn1 = own_half(dn1_term).astype(F32) + other_core(other_half(dn1_term)).astype(F32)
    x_own = tokens.astype(F32).reshape(block, width)
    inverse_own = lax.rsqrt(jnp.mean(x_own * x_own, axis=-1, keepdims=True) + EPS)
    grad_tokens = own_half(grad_hidden) + rms_backward(x_own, inverse_own, gain_attn, dn1)
    grad_tokens = grad_tokens.astype(BF).reshape(tokens.shape)

    kv_sums = jnp.sum(grad_kv.astype(F32), axis=0)
    kv_high = lax.reduce_precision(kv_sums, 8, 7)
    vectors = (
        grad_gain_attn,
        jnp.where(tp == 0, grad_gain_mlp, 0.0),
        jnp.sum(grad_query.astype(F32), axis=0),
        jnp.zeros((-inner % WIDE,), F32),
        kv_high,
        kv_sums - kv_high,
    )
    packed = jnp.concatenate([v.astype(BF) for v in vectors]).reshape(-1, WIDE)
    owners, lines = SIDE**3, packed.shape[0]
    own_kv = weight_grad(n1, grad_kv).astype(BF).reshape(owners, -1, WIDE)
    each = own_kv.shape[1]
    message = jnp.concatenate(
        [
            own_kv,
            jnp.broadcast_to(packed[None], (owners, *packed.shape)),
            jnp.zeros((owners, -(each + lines) % 8, WIDE), BF),
        ],
        axis=1,
    )
    message, weights, downs = lax.optimization_barrier((message, weights, downs))
    message = swap_and_sum(message, CTX)
    downs = sum_level(split(downs), FAR).astype(BF)
    weights = sum_level(split(weights), DEEP)
    downs = sum_level(split(downs), NEAR)
    message, weights, downs = lax.optimization_barrier((message, weights, downs))
    units = grad_gate.shape[1]
    mine, theirs = weights[:, :units], other_core(weights[:, units:])
    gate_shard, up_shard = jnp.where(first, mine, theirs), jnp.where(first, theirs, mine)
    down_shard = downs[:, :units].T
    output_shard = downs[:, units : units + inner].T
    query_shard = downs[:, units + inner :]
    kv_shard = message[:each]
    packed = message[each : each + lines]
    packed = jnp.concatenate([packed[:-2], packed[-2:-1] + packed[-1:]])
    packed_other = other_core(packed)
    both = packed + packed_other
    gains = both.reshape(-1)[: 2 * width]
    packed, packed_other = packed.reshape(-1)[2 * width :], packed_other.reshape(-1)[2 * width :]
    lower = jnp.where(tp == 0, packed, packed_other)
    upper = jnp.where(tp == 0, packed_other, packed)

    def both_cores(first, last):
        return jnp.concatenate([lower[first:last], upper[first:last]])

    keys_at = packed.shape[0] - WIDE
    return (
        mixed,
        grad_tokens,
        gains[:width],
        query_shard,
        both_cores(0, inner),
        kv_shard[:, :HEAD_DIM],
        both_cores(keys_at, keys_at + HEAD_DIM),
        kv_shard[:, HEAD_DIM:],
        both_cores(keys_at + HEAD_DIM, keys_at + WIDE),
        output_shard,
        gains[width:],
        gate_shard,
        up_shard,
        down_shard,
    )


def solution(mesh):
    split = Mesh(mesh.devices.reshape(SIDE, SIDE, SIDE, mesh.shape["tp"]), (*CTX, "tp"))
    return jax.shard_map(
        local,
        mesh=split,
        in_specs=(
            P(CTX, None, "tp", None),
            P(),
            P(None, "tp"),
            P("tp"),
            P(None, "tp"),
            P("tp"),
            P(None, "tp"),
            P("tp"),
            P("tp", None),
            P(),
            P(None, "tp"),
            P(None, "tp"),
            P("tp", None),
            P(CTX, None, "tp", None),
        ),
        out_specs=(
            P(CTX, None, "tp", None),
            P(CTX, None, "tp", None),
            P(),
            P(CTX, "tp"),
            P(),
            P(CTX, "tp"),
            P(),
            P(CTX, "tp"),
            P(),
            P("tp", CTX),
            P(),
            P(CTX, "tp"),
            P(CTX, "tp"),
            P("tp", CTX),
        ),
        check_vma=False,
    )
```

```python
import functools
import itertools

import jax
import jax.numpy as jnp
from jax import lax
from jax.experimental import pallas as pl
from jax.experimental.pallas import tpu as pltpu
from jax.sharding import Mesh
from jax.sharding import PartitionSpec as P

HEAD_DIM = 64
HEADS = 7
HALF = HEAD_DIM // 2
WIDE = 2 * HEAD_DIM
LANES = 640
CHUNK = 4
CTX = ("ctx_0", "ctx_1", "ctx_2")
ALL = (*CTX, "tp")
NEAR = ("ctx_0", "ctx_1")
FAR = ("ctx_1", "ctx_0")
DEEP = ("ctx_2", "ctx_2")
SIDE = 4
EPS = 1e-06
THETA = 1000000.0
NEG_FILL = -1e30
BF = jnp.bfloat16
F32 = jnp.float32


def columns_of(rows, group, block):
    parts = [
        rows[group * block : (group + 1) * block, h * HEAD_DIM : (h + 1) * HEAD_DIM]
        for h in range(HEADS)
    ]
    parts.append(jnp.zeros((LANES - HEADS * block, HEAD_DIM), rows.dtype))
    return jnp.concatenate(parts, axis=0)


def rows_of(columns, block):
    return jnp.concatenate(
        [columns[h * block : (h + 1) * block] for h in range(HEADS)], axis=1
    )


def slot_of(j, me_ref):
    s0 = (j // SIDE - me_ref[0]) & (SIDE - 1)
    s1 = (j % SIDE - me_ref[1]) & (SIDE - 1)
    return jnp.where(me_ref[3] == 0, s0 * SIDE + s1, s1 * SIDE + s0)


def causal(me2, late, block, query_row):
    shape = (CHUNK, block, LANES)
    b = lax.broadcasted_iota(jnp.int32, shape, 0).reshape(CHUNK * block, LANES)
    r = lax.broadcasted_iota(jnp.int32, shape, 1).reshape(CHUNK * block, LANES)
    ahead = (((b + me2) & (CHUNK - 1)) - me2) * block
    ahead = -ahead if late else ahead
    return ahead + r <= query_row


def forward_step(qt, kv, allowed, carry):
    top, acc = carry
    s = jnp.dot(kv, qt, preferred_element_type=F32)
    if allowed is not None:
        s = jnp.where(allowed, s, NEG_FILL)
    new = jnp.maximum(top, jnp.max(s, axis=0, keepdims=True))
    p = jnp.exp(s - new).astype(BF)
    shrink = jnp.exp(top - new)
    lane = lax.broadcasted_iota(jnp.int32, kv.shape, 1)
    ones_v = jnp.where(lane < HEAD_DIM, BF(1), kv)
    more = lax.dot_general(ones_v, p, (((0,), (0,)), ((), ())), preferred_element_type=F32)
    return new, acc * shrink + more


def no_keys_yet():
    return jnp.full((1, LANES), NEG_FILL, F32), jnp.zeros((WIDE, LANES), F32)


def first_kernel(q_ref, early_ref, cos_ref, sin_ref, qt_ref, top_ref, acc_ref):
    block = q_ref.shape[0] // 2
    for g in (0, 1):
        qt = columns_of(q_ref[...], g, block).T
        u, w = qt[:HALF], qt[HALF:]
        cos, sin = cos_ref[g], sin_ref[g]
        turned = jnp.concatenate([u * cos - w * sin, w * cos + u * sin], axis=0)
        qt_ref[g, :HEAD_DIM] = turned.astype(BF) * BF(0.125)
        qt_ref[g, HEAD_DIM:] = jnp.zeros((HEAD_DIM, LANES), BF)

    def step(slot, carry):
        return forward_step(qt_ref[1], early_ref[slot].reshape(-1, WIDE), None, carry)

    top_ref[...], acc_ref[...] = lax.fori_loop(
        0, early_ref.shape[0], step, no_keys_yet(), unroll=8
    )


def second_kernel(
    me_ref,
    qt_ref,
    top_ref,
    acc_ref,
    early_ref,
    late_ref,
    row_ref,
    ot_ref,
    lse_ref,
    att_ref,
    tops_ref,
    accs_ref,
):
    block = early_ref.shape[2]
    mine = me_ref[0] * SIDE + me_ref[1]
    tops_ref[0], accs_ref[0] = no_keys_yet()
    tops_ref[1], accs_ref[1] = top_ref[...], acc_ref[...]

    def step(i, unused):
        late = i >= mine
        g = late.astype(jnp.int32)
        slot = slot_of(jnp.where(late, i + 1, i), me_ref)
        kv = jnp.where(late, late_ref[slot], early_ref[slot]).reshape(-1, WIDE)
        tops_ref[g], accs_ref[g] = forward_step(
            qt_ref[g], kv, None, (tops_ref[g], accs_ref[g])
        )
        return unused

    lax.fori_loop(0, early_ref.shape[0] - 1, step, 0, unroll=5)
    for g, ref in enumerate((early_ref, late_ref)):
        allowed = causal(me_ref[2], g == 1, block, row_ref[...])
        carry = (tops_ref[g], accs_ref[g])
        top, acc = forward_step(qt_ref[g], ref[0].reshape(-1, WIDE), allowed, carry)
        total = acc[0:1]
        out = acc[HEAD_DIM:] / total
        ot_ref[g] = out
        lse_ref[g] = top + jnp.log(total)
        att_ref[g * block : (g + 1) * block] = rows_of(out.T, block).astype(BF)


def backward_operands(g, qt_ref, ot_ref, lse_ref, grad_ref):
    block = grad_ref.shape[0] // 2
    qt = qt_ref[g]
    grad = columns_of(grad_ref[...].astype(F32), g, block)
    none = jnp.zeros((LANES, HEAD_DIM), F32)
    grad_rows = jnp.concatenate([none, grad], axis=1)
    grad_t = grad_rows.T
    delta = jnp.sum(grad_t[HEAD_DIM:] * ot_ref[g], axis=0, keepdims=True)
    q_rows = qt.astype(F32).T.astype(BF)
    return qt, q_rows, grad_t.astype(BF), grad_rows.astype(BF), lse_ref[g], delta


def backward_step(operands, kv, allowed):
    qt, q_rows, grad_t, grad_rows, lse, delta = operands
    s = jnp.dot(kv, qt, preferred_element_type=F32)
    p = jnp.exp(s - lse)
    if allowed is not None:
        p = jnp.where(allowed, p, 0.0)
    dp = jnp.dot(kv, grad_t, preferred_element_type=F32)
    ds = (p * (dp - delta)).astype(BF)
    dkv = jnp.dot(ds, q_rows, preferred_element_type=F32) + jnp.dot(
        p.astype(BF), grad_rows, preferred_element_type=F32
    )
    dqt = lax.dot_general(kv, ds, (((0,), (0,)), ((), ())), preferred_element_type=F32)
    return dkv, dqt


def back_first_kernel(qt_ref, ot_ref, lse_ref, grad_ref, early_ref, dqt_ref, sum_ref):
    keys = CHUNK * early_ref.shape[2]
    operands = backward_operands(1, qt_ref, ot_ref, lse_ref, grad_ref)

    def step(slot, dqt):
        dkv, more = backward_step(operands, early_ref[slot].reshape(keys, WIDE), None)
        sum_ref[slot] = dkv.reshape(sum_ref.shape[1:])
        return dqt + more

    start = jnp.zeros((WIDE, LANES), F32)
    dqt_ref[...] = lax.fori_loop(0, early_ref.shape[0], step, start, unroll=8)


def back_second_kernel(
    me_ref,
    qt_ref,
    ot_ref,
    lse_ref,
    grad_ref,
    early_ref,
    late_ref,
    cos_ref,
    sin_ref,
    row_ref,
    dqt_ref,
    sum_ref,
    *rest,
):
    scratch, rest = rest[-6:], rest[:-6]
    dq_ref, out_refs = rest[-1 - SIDE], rest[-SIDE:]
    q_rows_ref, grad_t_ref, grad_rows_ref, delta_ref, dqts_ref, dkv_ref = scratch
    block = grad_ref.shape[0] // 2
    keys = CHUNK * block
    mine = me_ref[0] * SIDE + me_ref[1]
    for g in (0, 1):
        unused, q_rows, grad_t, grad_rows, unused, delta = backward_operands(
            g, qt_ref, ot_ref, lse_ref, grad_ref
        )
        q_rows_ref[g], grad_t_ref[g], grad_rows_ref[g] = q_rows, grad_t, grad_rows
        delta_ref[g] = delta

    def operands(g):
        return (
            qt_ref[g],
            q_rows_ref[g],
            grad_t_ref[g],
            grad_rows_ref[g],
            lse_ref[g],
            delta_ref[g],
        )

    def put(slot, part, dkv):
        dkv_ref[slot, :, part] = dkv.reshape(CHUNK, block, WIDE).astype(BF)

    dqts_ref[0] = jnp.zeros((WIDE, LANES), F32)
    dqts_ref[1] = dqt_ref[...]

    def step(i, unused):
        late = i >= mine
        g = late.astype(jnp.int32)
        slot = slot_of(jnp.where(late, i + 1, i), me_ref)
        kv = jnp.where(late, late_ref[slot], early_ref[slot]).reshape(keys, WIDE)
        dkv, more = backward_step(operands(g), kv, None)
        put(slot, 0, sum_ref[slot].reshape(keys, WIDE) + jnp.where(late, 0.0, dkv))
        put(slot, 1, jnp.where(late, dkv, 0.0))
        dqts_ref[g] += more
        return unused

    lax.fori_loop(0, early_ref.shape[0] - 1, step, 0, unroll=5)
    for g, ref in enumerate((early_ref, late_ref)):
        allowed = causal(me_ref[2], g == 1, block, row_ref[...])
        dkv, more = backward_step(operands(g), ref[0].reshape(keys, WIDE), allowed)
        put(0, g, dkv + sum_ref[0].reshape(keys, WIDE) if g == 0 else dkv)
        dqt = dqts_ref[g] + more
        u, w = dqt[:HALF] * 0.125, dqt[HALF:HEAD_DIM] * 0.125
        cos, sin = cos_ref[g], sin_ref[g]
        dq = jnp.concatenate([u * cos + w * sin, w * cos - u * sin], axis=0).T
        dq_ref[g * block : (g + 1) * block] = rows_of(dq, block).astype(dq_ref.dtype)
    for k, out_ref in enumerate(out_refs):
        out_ref[...] = dkv_ref[k * SIDE : (k + 1) * SIDE]


VMEM = pl.BlockSpec(memory_space=pltpu.VMEM)
SMEM = pl.BlockSpec(memory_space=pltpu.SMEM)
PARAMS = pltpu.CompilerParams(vmem_limit_bytes=28 * 1024 * 1024)


def attend_first(q, early, cos, sin):
    return pl.pallas_call(
        first_kernel,
        out_shape=(
            jax.ShapeDtypeStruct((2, WIDE, LANES), BF),
            jax.ShapeDtypeStruct((1, LANES), F32),
            jax.ShapeDtypeStruct((WIDE, LANES), F32),
        ),
        in_specs=[VMEM] * 4,
        out_specs=(VMEM,) * 3,
        compiler_params=PARAMS,
        cost_estimate=pl.CostEstimate(
            flops=13_000_000_000, bytes_accessed=2_000_000, transcendentals=0
        ),
        name="attend_first",
    )(q, early, cos, sin)


def attend_second(me, qt, top, acc, early, late, rows):
    own = 2 * early.shape[2]
    return pl.pallas_call(
        second_kernel,
        out_shape=(
            jax.ShapeDtypeStruct((2, HEAD_DIM, LANES), F32),
            jax.ShapeDtypeStruct((2, 1, LANES), F32),
            jax.ShapeDtypeStruct((own, HEADS * HEAD_DIM), BF),
        ),
        in_specs=[SMEM] + [VMEM] * 6,
        out_specs=(VMEM,) * 3,
        scratch_shapes=[pltpu.VMEM((2, 1, LANES), F32), pltpu.VMEM((2, WIDE, LANES), F32)],
        compiler_params=PARAMS,
        cost_estimate=pl.CostEstimate(
            flops=13_000_000_000, bytes_accessed=2_000_000, transcendentals=0
        ),
        name="attend_second",
    )(me, qt, top, acc, early, late, rows)


def attend_back_first(qt, ot, lse, grad, early):
    return pl.pallas_call(
        back_first_kernel,
        out_shape=(
            jax.ShapeDtypeStruct((WIDE, LANES), F32),
            jax.ShapeDtypeStruct(early.shape, F32),
        ),
        in_specs=[VMEM] * 5,
        out_specs=(VMEM,) * 2,
        compiler_params=PARAMS,
        cost_estimate=pl.CostEstimate(
            flops=14_000_000_000, bytes_accessed=4_000_000, transcendentals=0
        ),
        name="attend_back_first",
    )(qt, ot, lse, grad, early)


def attend_back_second(me, qt, ot, lse, grad, early, late, cos, sin, rows, dqt, sums, before):
    own = grad.shape[0]
    part = (SIDE, CHUNK, 2, *early.shape[2:])
    return pl.pallas_call(
        back_second_kernel,
        out_shape=(
            jax.ShapeDtypeStruct((own, HEADS * HEAD_DIM), BF),
            *[jax.ShapeDtypeStruct(part, BF)] * SIDE,
        ),
        in_specs=[SMEM] + [VMEM] * 11 + [pl.BlockSpec(memory_space=pl.ANY)] * len(before),
        out_specs=(VMEM,) * (1 + SIDE),
        scratch_shapes=[
            pltpu.VMEM((2, LANES, WIDE), BF),
            pltpu.VMEM((2, WIDE, LANES), BF),
            pltpu.VMEM((2, LANES, WIDE), BF),
            pltpu.VMEM((2, 1, LANES), F32),
            pltpu.VMEM((2, WIDE, LANES), F32),
            pltpu.VMEM((SIDE * part[0], *part[1:]), BF),
        ],
        compiler_params=PARAMS,
        cost_estimate=pl.CostEstimate(
            flops=14_000_000_000, bytes_accessed=8_000_000, transcendentals=0
        ),
        name="attend_back_second",
    )(me, qt, ot, lse, grad, early, late, cos, sin, rows, dqt, sums, *before)


def send(array, axes, s):
    pairs = []
    for source in itertools.product(range(SIDE), range(SIDE), range(SIDE), range(2)):
        target = list(source)
        k = CTX.index(axes[source[3]])
        target[k] = (target[k] + s) % SIDE
        pairs.append((linear(source), linear(target)))
    return lax.ppermute(array, ALL, pairs)


def linear(place):
    return ((place[0] * SIDE + place[1]) * SIDE + place[2]) * 2 + place[3]


def fetch(array, axes, s):
    return send(array, axes, SIDE - s)


def other_core(array):
    return lax.ppermute(array, "tp", [(0, 1), (1, 0)])


def gather(array, axes, dim):
    return jnp.stack([array] + [fetch(array, axes, s) for s in range(1, SIDE)], axis=dim)


def total_of(arrays):
    total = arrays[0].astype(F32)
    for a in arrays[1:]:
        total = total + a.astype(F32)
    return total


def sum_level(pieces, axes):
    return total_of([pieces[0]] + [send(pieces[s], axes, s) for s in range(1, SIDE)])


def split(array):
    rows = array.shape[0] // SIDE
    return [array[s * rows : (s + 1) * rows] for s in range(SIDE)]


def swap_and_sum(blocks, axes):
    return jnp.sum(lax.all_to_all(blocks, axes, 0, 0, tiled=True).astype(F32), axis=0)


def by_distance(me, levels, width):
    each = width // SIDE**3
    place = jnp.arange(width)
    part, within = place // each, place % each
    parts = jnp.stack([part // SIDE**2, part // SIDE % SIDE, part % SIDE])
    d0, d1, d2 = [(me[k] + parts[levels[k]]) % SIDE for k in range(3)]
    feature = ((d0 * SIDE + d1) * SIDE + d2) * each + within
    return (jnp.arange(width)[:, None] == feature[None, :]).astype(BF)


def rearranged(rows, table):
    return jnp.dot(rows, table, preferred_element_type=F32).astype(BF)


def weight_grad(rows, grads):
    return lax.dot_general(rows, grads, (((0,), (0,)), ((), ())), preferred_element_type=F32)


def columns(rows):
    size = rows.shape[1] // SIDE
    return [rows[:, s * size : (s + 1) * size] for s in range(SIDE)]


class Ring:
    def __init__(self, rows, grads, axes):
        self.axes, self.grads = axes, grads
        self.rows = columns(rows)
        half = self.rows[0].shape[1] // 2
        self.far = weight_grad(self.rows[2], grads).astype(BF)
        self.between = [
            send(self.far[:half], axes, 1),
            send(self.far[half:], axes, SIDE - 1),
        ]

    def second(self, beside=None):
        none = jnp.zeros(self.between[0].shape, F32)
        right = weight_grad(self.rows[1], self.grads) + jnp.concatenate(
            [self.between[0].astype(F32), none], axis=0
        )
        left = weight_grad(self.rows[3], self.grads) + jnp.concatenate(
            [none, self.between[1].astype(F32)], axis=0
        )
        right, left = right.astype(BF), left.astype(BF)
        if beside is not None:
            right = jnp.concatenate([right, beside[1]], axis=1)
            left = jnp.concatenate([left, beside[3]], axis=1)
        self.arrived = [send(right, self.axes, 1), send(left, self.axes, SIDE - 1)]
        return [right, left]

    def total(self):
        width = self.grads.shape[1]
        arrived = [a[:, :width] for a in self.arrived]
        return total_of([weight_grad(self.rows[0], self.grads), *arrived]).astype(BF)


def rms_forward(rows, gain):
    inverse = lax.rsqrt(jnp.mean(rows * rows, axis=-1, keepdims=True) + EPS)
    return (rows * inverse * gain, inverse)


def rms_backward(rows, inverse, gain, grad_out):
    weighted = grad_out * gain
    inner = jnp.mean(rows * weighted, axis=-1, keepdims=True)
    return inverse * weighted - rows * (inverse * inverse * inverse) * inner


def angles(positions):
    freqs = 1.0 / THETA ** (jnp.arange(0, HEAD_DIM, 2).astype(F32) / HEAD_DIM)
    return positions.astype(F32), freqs


def local(
    tokens,
    gain_attn,
    query_projection_weight,
    query_bias_vector,
    key_projection_weight,
    key_bias_vector,
    value_projection_weight,
    value_bias_vector,
    w_output,
    gain_mlp,
    w_gate,
    w_up,
    w_down,
    cotangent,
):
    me = [lax.axis_index(a) for a in CTX]
    tp = lax.axis_index("tp")
    ctx_count = SIDE**3
    ctx = (me[0] * SIDE + me[1]) * SIDE + me[2]
    half = tokens.shape[2]
    block = 2 * half
    width = tokens.shape[3]
    own = 2 * block
    places = jnp.stack([me[0], me[1], me[2], tp]).astype(jnp.int32)

    def both_halves(array):
        mine = array.reshape(2, half, width)
        theirs = other_core(mine)
        halves = [jnp.where(tp == 0, mine, theirs), jnp.where(tp == 0, theirs, mine)]
        return jnp.stack(halves, axis=1).reshape(own, width)

    def own_half(array):
        return lax.dynamic_index_in_dim(
            array.reshape(2, 2, half, width), tp, 1, keepdims=False
        ).reshape(block, width)

    def other_half(array):
        return lax.dynamic_index_in_dim(
            array.reshape(2, 2, half, width), 1 - tp, 1, keepdims=False
        ).reshape(block, width)

    firsts = jnp.stack([ctx * block, (2 * ctx_count - 1 - ctx) * block])
    row = jnp.arange(LANES) % block
    row = jnp.where(jnp.arange(LANES) < HEADS * block, row, 0)
    lane_places, freqs = angles(firsts[:, None] + row[None, :])
    lane_angles = lane_places[:, None, :] * freqs[None, :, None]
    lane_cos, lane_sin = jnp.cos(lane_angles), jnp.sin(lane_angles)
    own_places, freqs = angles((firsts[:, None] + jnp.arange(block)[None, :]).reshape(-1))
    own_angles = own_places[:, None] * freqs[None, :]
    cos, sin = jnp.cos(own_angles), jnp.sin(own_angles)
    query_row = row.astype(jnp.int32)[None, :]

    x_all = lax.all_gather(tokens.reshape(2, half, width), "tp", axis=0)
    x_all = jnp.moveaxis(x_all, 0, 1).reshape(own, width).astype(F32)
    dy_all = both_halves(cotangent)
    n1, inverse_attn = rms_forward(x_all, gain_attn)
    n1 = n1.astype(BF)
    key_pre = jnp.dot(n1, key_projection_weight, preferred_element_type=F32) + key_bias_vector
    value_pre = jnp.dot(n1, value_projection_weight, preferred_element_type=F32) + value_bias_vector
    u, w = key_pre[:, :HALF], key_pre[:, HALF:]
    kv_own = jnp.concatenate([u * cos - w * sin, w * cos + u * sin, value_pre], axis=1)
    kv_own = kv_own.astype(BF).reshape(2, block, WIDE)
    kv_row = gather(kv_own, DEEP, 1)
    shape = (SIDE * SIDE, CHUNK, block, WIDE)
    early_row = gather(kv_row[0], FAR, 0)
    early = gather(early_row, NEAR, 0).reshape(shape)
    late_row = gather(kv_row[1], FAR, 0)
    late_rows = [fetch(late_row, NEAR, 1)]

    query_pre = (
        jnp.dot(n1, query_projection_weight, preferred_element_type=F32) + query_bias_vector
    )
    near_first = by_distance(me, (tp, 1 - tp, 2), width)
    deep_first = by_distance(me, (2 - tp, 1 + tp, 0), width)
    grad_act = jnp.einsum("rd,fd->rf", dy_all, w_down, preferred_element_type=F32)
    dy_deep = rearranged(dy_all, deep_first)
    n1_deep = rearranged(n1, deep_first)

    early, late_row, grad_act = lax.optimization_barrier((early, late_row, grad_act))
    late_rows += [fetch(late_row, NEAR, s) for s in range(2, SIDE)]
    qt, top, acc = attend_first(query_pre, early, lane_cos, lane_sin)
    top, acc, *late_rows = lax.optimization_barrier((top, acc, *late_rows))
    late = jnp.stack([late_row, *late_rows]).reshape(shape)
    ot, lse, attended = attend_second(places, qt, top, acc, early, late, query_row)
    attn_term = jnp.dot(attended, w_output, preferred_element_type=F32).astype(BF)
    attn_rows = attn_term.astype(F32) + other_core(attn_term).astype(F32)
    hidden = x_all + attn_rows

    n2, inverse_mlp = rms_forward(hidden, gain_mlp)
    n2 = n2.astype(BF)
    gate_rows = jnp.dot(n2, w_gate, preferred_element_type=F32)
    up_rows = jnp.dot(n2, w_up, preferred_element_type=F32)
    sigmoid_gate = jax.nn.sigmoid(gate_rows)
    silu_gate = gate_rows * sigmoid_gate
    activation = (silu_gate * up_rows).astype(BF)
    grad_gate = (
        grad_act * up_rows * sigmoid_gate * (1.0 + gate_rows * (1.0 - sigmoid_gate))
    ).astype(BF)
    grad_up = (grad_act * silu_gate).astype(BF)
    first = tp == 0
    kept = jnp.where(first, grad_gate, grad_up)
    given = other_core(jnp.where(first, grad_up, grad_gate))
    down_ring = Ring(dy_deep, activation, DEEP)
    grad_gate, grad_up, unused = lax.optimization_barrier((grad_gate, grad_up, down_ring.far))
    dn2_term = (
        jnp.einsum("rf,df->rd", grad_gate, w_gate, preferred_element_type=F32)
        + jnp.einsum("rf,df->rd", grad_up, w_up, preferred_element_type=F32)
    ).astype(BF)
    dn2_other = other_core(dn2_term)
    ring = Ring(rearranged(n2, near_first), jnp.concatenate([kept, given], axis=1), NEAR)
    dn2 = dn2_term.astype(F32) + dn2_other.astype(F32)
    grad_hidden = dy_all.astype(F32) + rms_backward(hidden, inverse_mlp, gain_mlp, dn2)
    grad_gain_mlp = jnp.sum(dn2 * hidden * inverse_mlp, axis=0)
    grad_attn = grad_hidden.astype(BF)
    grad_attended = jnp.einsum(
        "rd,qd->rq", grad_attn, w_output, preferred_element_type=F32
    ).astype(BF)
    output_pieces = [
        weight_grad(r, attended).astype(BF) for r in columns(rearranged(grad_attn, deep_first))
    ]

    dqt, sums = attend_back_first(qt, ot, lse, grad_attended, early)
    dqt, *between = lax.optimization_barrier((dqt, *ring.between, *down_ring.between))
    ring.between, down_ring.between = between[:2], between[2:]
    before = [*output_pieces, *down_ring.second(output_pieces), *ring.second()]
    grad_query, *grad_kv = attend_back_second(
        places, qt, ot, lse, grad_attended, early, late, lane_cos, lane_sin, query_row, dqt, sums, before
    )
    grad_query, activation, *held = lax.optimization_barrier(
        (grad_query, activation, *grad_kv, *down_ring.arrived)
    )
    grad_kv, down_ring.arrived = held[:SIDE], held[SIDE:]

    inner = HEADS * HEAD_DIM
    output_far = send(output_pieces[2], DEEP, 2)
    grad_kv = [part.reshape(-1, block, WIDE) for part in grad_kv]
    grad_kv = sum_level(grad_kv, NEAR).astype(BF)
    query_pieces = [weight_grad(r, grad_query).astype(BF) for r in columns(n1_deep)]
    grad_kv, *held = lax.optimization_barrier((grad_kv, *ring.arrived, *query_pieces))
    ring.arrived, query_pieces = held[:2], held[2:]
    grad_kv = sum_level(split(grad_kv), FAR).astype(BF)
    query_near = sum_level(query_pieces, DEEP).astype(BF)
    output_near = [output_pieces[0], output_far] + [a[:, -inner:] for a in down_ring.arrived]
    output_near = total_of(output_near).astype(BF)
    downs = jnp.concatenate([down_ring.total(), output_near, query_near], axis=1)
    grad_kv, weights = lax.optimization_barrier((grad_kv, ring.total()))
    grad_kv = sum_level(split(grad_kv), DEEP)
    mlp_term = jnp.dot(activation, w_down, preferred_element_type=F32).astype(BF)
    mlp_rows = own_half(mlp_term).astype(F32) + other_core(other_half(mlp_term)).astype(F32)
    mixed = (own_half(hidden) + mlp_rows).astype(BF).reshape(tokens.shape)

    weights = sum_level(split(weights), FAR).astype(BF)
    grad_kv, mixed = lax.optimization_barrier((grad_kv, mixed))
    grad_kv = grad_kv.reshape(own, WIDE)
    u, w = grad_kv[:, :HALF], grad_kv[:, HALF:HEAD_DIM]
    grad_kv = jnp.concatenate(
        [u * cos + w * sin, w * cos - u * sin, grad_kv[:, HEAD_DIM:]], axis=1
    ).astype(BF)

    dn1_term = jnp.einsum(
        "rq,dq->rd", grad_query, query_projection_weight, preferred_element_type=F32
    )
    kv_weight = jnp.concatenate([key_projection_weight, value_projection_weight], axis=1)
    dn1_term = dn1_term + jnp.einsum("rq,dq->rd", grad_kv, kv_weight, preferred_element_type=F32)
    grad_gain_attn = jnp.sum(dn1_term * x_all * inverse_attn, axis=0)
    dn1_term = dn1_term.astype(BF)
    dn1 = own_half(dn1_term).astype(F32) + other_core(other_half(dn1_term)).astype(F32)
    x_own = tokens.astype(F32).reshape(block, width)
    inverse_own = lax.rsqrt(jnp.mean(x_own * x_own, axis=-1, keepdims=True) + EPS)
    grad_tokens = own_half(grad_hidden) + rms_backward(x_own, inverse_own, gain_attn, dn1)
    grad_tokens = grad_tokens.astype(BF).reshape(tokens.shape)

    kv_sums = jnp.sum(grad_kv.astype(F32), axis=0)
    kv_high = lax.reduce_precision(kv_sums, 8, 7)
    vectors = (
        grad_gain_attn,
        jnp.where(tp == 0, grad_gain_mlp, 0.0),
        jnp.sum(grad_query.astype(F32), axis=0),
        jnp.zeros((-inner % WIDE,), F32),
        kv_high,
        kv_sums - kv_high,
    )
    packed = jnp.concatenate([v.astype(BF) for v in vectors]).reshape(-1, WIDE)
    owners, lines = SIDE**3, packed.shape[0]
    own_kv = weight_grad(n1, grad_kv).astype(BF).reshape(owners, -1, WIDE)
    each = own_kv.shape[1]
    message = jnp.concatenate(
        [
            own_kv,
            jnp.broadcast_to(packed[None], (owners, *packed.shape)),
            jnp.zeros((owners, -(each + lines) % 8, WIDE), BF),
        ],
        axis=1,
    )
    message, weights, downs = lax.optimization_barrier((message, weights, downs))
    message = swap_and_sum(message, CTX)
    downs = sum_level(split(downs), FAR).astype(BF)
    weights = sum_level(split(weights), DEEP)
    downs = sum_level(split(downs), NEAR)
    message, weights, downs = lax.optimization_barrier((message, weights, downs))
    units = grad_gate.shape[1]
    mine, theirs = weights[:, :units], other_core(weights[:, units:])
    gate_shard, up_shard = jnp.where(first, mine, theirs), jnp.where(first, theirs, mine)
    down_shard = downs[:, :units].T
    output_shard = downs[:, units : units + inner].T
    query_shard = downs[:, units + inner :]
    kv_shard = message[:each]
    packed = message[each : each + lines]
    packed = jnp.concatenate([packed[:-2], packed[-2:-1] + packed[-1:]])
    packed_other = other_core(packed)
    both = packed + packed_other
    gains = both.reshape(-1)[: 2 * width]
    packed, packed_other = packed.reshape(-1)[2 * width :], packed_other.reshape(-1)[2 * width :]
    lower = jnp.where(tp == 0, packed, packed_other)
    upper = jnp.where(tp == 0, packed_other, packed)

    def both_cores(first, last):
        return jnp.concatenate([lower[first:last], upper[first:last]])

    keys_at = packed.shape[0] - WIDE
    return (
        mixed,
        grad_tokens,
        gains[:width],
        query_shard,
        both_cores(0, inner),
        kv_shard[:, :HEAD_DIM],
        both_cores(keys_at, keys_at + HEAD_DIM),
        kv_shard[:, HEAD_DIM:],
        both_cores(keys_at + HEAD_DIM, keys_at + WIDE),
        output_shard,
        gains[width:],
        gate_shard,
        up_shard,
        down_shard,
    )


def solution(mesh):
    split = Mesh(mesh.devices.reshape(SIDE, SIDE, SIDE, mesh.shape["tp"]), (*CTX, "tp"))
    return jax.shard_map(
        local,
        mesh=split,
        in_specs=(
            P(CTX, None, "tp", None),
            P(),
            P(None, "tp"),
            P("tp"),
            P(None, "tp"),
            P("tp"),
            P(None, "tp"),
            P("tp"),
            P("tp", None),
            P(),
            P(None, "tp"),
            P(None, "tp"),
            P("tp", None),
            P(CTX, None, "tp", None),
        ),
        out_specs=(
            P(CTX, None, "tp", None),
            P(CTX, None, "tp", None),
            P(),
            P(CTX, "tp"),
            P(),
            P(CTX, "tp"),
            P(),
            P(CTX, "tp"),
            P(),
            P("tp", CTX),
            P(),
            P(CTX, "tp"),
            P(CTX, "tp"),
            P("tp", CTX),
        ),
        check_vma=False,
    )
```
